128 devices in a mesh: stu: 8 (over y, core), tea: 16 (over z, x).
Axes of the slice: x: 4, y: 4, z: 4, core: 2. Of those that a mesh axis runs over, the one named last changes fastest.
Arguments:
- student: bfloat16 [16384, 2048], P('stu', 'tea'), may hold values from -8 to 8
- teacher: bfloat16 [16384, 2048], P('tea', 'stu'), may hold values from -8 to 8
- band_start: int32 [32], replicated, may hold values from 0 to 28, as said below
Outputs:
- grad_student: float32 [16384, 2048], P('stu', 'tea')
- stu_pot: float32 [16384], P('stu')
- tea_pot: float32 [16384], P('tea')
- loss: float32 [], replicated
The draws below stay inside these ranges and needn't reach their ends.
Inputs may be any that keep to these rules, and one draw needn't show every extreme that they name: student block a is paired with teacher blocks band_start[a] to band_start[a] + 3; every teacher block is paired with at least one student block, block 0 with student block 0.
All inputs are finite; a program needn't handle non-finite values.
Results may differ from the reference program's by a relative error of at most 0.002.
Values may be sent and summed in bfloat16 or wider, within the bound.
A program may use at most 192 MiB of HBM per device.

```python
import math
import jax
import jax.numpy as jnp
from jax import lax

D = 2048
BLK = 512
W = 4
ITERS = 3
NB = 32
S = 16384


def draw_student(key, part):
    key = jax.random.fold_in(key, 11)
    first = jax.random.fold_in(key, 0)
    values = jnp.clip(jax.random.normal(first, (S, D), jnp.float32), -6.0, 6.0)
    return values.astype(jnp.bfloat16)


def draw_teacher(key, part):
    key = jax.random.fold_in(key, 23)
    first = jax.random.fold_in(key, 0)
    values = jnp.clip(jax.random.normal(first, (S, D), jnp.float32), -6.0, 6.0)
    return values.astype(jnp.bfloat16)


def draw_band_start(key, part):
    key = jax.random.fold_in(key, 31)
    placing_key = jax.random.fold_in(key, 1)
    spread_key = jax.random.fold_in(key, 2)
    placing = jax.random.permutation(placing_key, NB - 1).astype(jnp.int32) + 1
    covering = (NB + W - 1) // W
    position = jnp.arange(NB - 1, dtype=jnp.int32)
    spread_start = jax.random.randint(spread_key, (NB - 1,), 0, NB - W + 1).astype(jnp.int32)
    chosen = jnp.where(position < covering - 1, jnp.minimum((position + 1) * W, NB - W), spread_start)
    return jnp.zeros((NB,), jnp.int32).at[placing].set(chosen.astype(jnp.int32))


def setup_inputs(seed: int = 0) -> dict:
    splits = jax.random.split(jax.random.key(seed), 4)
    return {
        "student": draw_student(jax.random.fold_in(splits[3], 71), 0),
        "teacher": draw_teacher(jax.random.fold_in(splits[3], 71), 0),
        "band_start": draw_band_start(jax.random.fold_in(splits[3], 71), 0),
    }


epsilon = 0.02


def squares(rows):
    return jnp.sum(jnp.square(rows.astype(jnp.float32)), axis=1)


def reference(student, teacher, band_start):
    blocks = S // BLK
    window = W * BLK
    offsets = (band_start * BLK).astype(jnp.int32)
    columns = offsets[:, None] + jnp.arange(window, dtype=jnp.int32)[None, :]

    def block_cost(index):
        rows = lax.dynamic_slice_in_dim(student, (index * BLK).astype(jnp.int32), BLK, 0)
        others = lax.dynamic_slice_in_dim(teacher, offsets[index], window, 0)
        inner = jnp.dot(rows, others.T, preferred_element_type=jnp.float32)
        return (squares(rows)[:, None] + squares(others)[None, :] - 2.0 * inner) / D

    tile_cost = lax.map(block_cost, jnp.arange(blocks, dtype=jnp.int32))
    log_marginal = -math.log(S)
    tea_pot = jnp.zeros((S,), jnp.float32)
    stu_pot = jnp.zeros((S,), jnp.float32)
    for sweep in range(ITERS):
        scores = (tea_pot[columns][:, None, :] - tile_cost) / epsilon
        stu_pot = epsilon * log_marginal - epsilon * jax.nn.logsumexp(scores, axis=2).reshape(S)
        scores = (stu_pot.reshape(blocks, BLK, 1) - tile_cost) / epsilon
        col_peak = jnp.full((S,), -jnp.inf, jnp.float32).at[columns].max(jnp.max(scores, axis=1))
        shifted = jnp.exp(scores - col_peak[columns][:, None, :])
        col_total = jnp.zeros((S,), jnp.float32).at[columns].add(jnp.sum(shifted, axis=1))
        tea_pot = epsilon * log_marginal - epsilon * (col_peak + jnp.log(col_total))
    transport = jnp.exp((stu_pot.reshape(blocks, BLK, 1) + tea_pot[columns][:, None, :] - tile_cost) / epsilon)
    loss = jnp.sum(transport * tile_cost)
    weights = (transport * S).astype(jnp.bfloat16)
    row_mass = jnp.sum(weights.astype(jnp.float32), axis=2).reshape(S)

    def block_pull(index):
        others = lax.dynamic_slice_in_dim(teacher, offsets[index], window, 0)
        return jnp.dot(weights[index], others, preferred_element_type=jnp.float32)

    pulled = lax.map(block_pull, jnp.arange(blocks, dtype=jnp.int32)).reshape(S, D)
    grad_student = row_mass[:, None] * student.astype(jnp.float32) - pulled
    return (grad_student, stu_pot, tea_pot, loss)
```

```python
import functools
import math

import jax
import jax.numpy as jnp
from jax import lax
from jax.experimental import pallas as pl
from jax.experimental.pallas import tpu as pltpu
from jax.sharding import PartitionSpec as P

D = 2048
BLK = 512
W = 4
ITERS = 3
LANES = 128

epsilon = 0.02
kappa = math.log2(math.e) / epsilon
log2e = math.log2(math.e)
unlisted = -1e30
MESH = pl.DeviceIdType.MESH


def diagonal():
    rows = lax.broadcasted_iota(jnp.int32, (LANES, LANES), 0)
    cols = lax.broadcasted_iota(jnp.int32, (LANES, LANES), 1)
    return rows == cols


def to_lanes(column):
    return jnp.sum(jnp.where(diagonal(), column, 0.0), axis=0, keepdims=True)


def to_sublanes(row):
    return jnp.sum(jnp.where(diagonal(), row, 0.0), axis=1, keepdims=True)


def merge(parts):
    highest = functools.reduce(jnp.maximum, [m for m, _ in parts])
    total = functools.reduce(
        lambda a, b: a + b, [s * jnp.exp2(m - highest) for m, s in parts]
    )
    return highest, total


def row_stats(z_ref, tea_ref, put):
    rows_total = z_ref.shape[0]
    pot = tea_ref[...]

    def block(b, carry):
        highs, sums = [], []
        for part in range(4):
            first = pl.multiple_of(b * LANES + part * 32, 32)
            scores = z_ref[pl.ds(first, 32), :] + pot
            high = jnp.max(scores, axis=1, keepdims=True)
            highs.append(high)
            sums.append(jnp.sum(jnp.exp2(scores - high), axis=1, keepdims=True))
        put(
            b,
            to_lanes(jnp.concatenate(highs, axis=0)),
            to_lanes(jnp.concatenate(sums, axis=0)),
        )
        return carry

    lax.fori_loop(0, rows_total // LANES, block, 0)


def spread_rows(compact_ref, wide_ref):
    def block(b, carry):
        column = to_sublanes(compact_ref[pl.ds(b, 1), :])
        rows = pl.ds(pl.multiple_of(b * LANES, LANES), LANES)
        wide_ref[rows, :] = jnp.broadcast_to(column, (LANES, LANES))
        return carry

    lax.fori_loop(0, compact_ref.shape[0], block, 0)


def col_stats(z_ref, wide_ref, put):
    rows_total, cols = z_ref.shape
    tiles = cols // LANES

    def block(b, carry):
        rows = pl.ds(pl.multiple_of(b * LANES, LANES), LANES)
        pot = wide_ref[rows, :]
        out = []
        for c in range(tiles):
            high, total = carry[c]
            scores = z_ref[rows, c * LANES:(c + 1) * LANES] + pot
            scores = scores.reshape(LANES // 8, 8, LANES)
            new = jnp.maximum(high, jnp.max(scores, axis=0))
            total = total * jnp.exp2(high - new) + jnp.sum(jnp.exp2(scores - new[None]), axis=0)
            out.append((new, total))
        return tuple(out)

    start = tuple(
        (jnp.full((8, LANES), unlisted, jnp.float32), jnp.zeros((8, LANES), jnp.float32))
        for _ in range(tiles)
    )
    done = lax.fori_loop(0, rows_total // LANES, block, start)
    for c, (high, total) in enumerate(done):
        top = jnp.max(high, axis=0, keepdims=True)
        put(c, top, jnp.sum(total * jnp.exp2(high - top), axis=0, keepdims=True))


def places():
    s = lax.axis_index("stu")
    t = lax.axis_index("tea")
    return s, t, lax.div(t, 4), lax.rem(t, 4)


def peers_x(d):
    s, t, z, x = places()
    return (s, z * 4 + lax.rem(x + d, 4))


def peers_z(d):
    s, t, z, x = places()
    return (s, lax.rem(z + d, 4) * 4 + x)


def peers_s(d):
    s, t, z, x = places()
    return (lax.rem(s + d, 8), t)


def exchange(source, landing, send, recv, peer, count):
    copies = []
    for d in range(1, count):
        copies.append(
            pltpu.make_async_remote_copy(
                src_ref=source,
                dst_ref=landing.at[d - 1],
                send_sem=send.at[d - 1],
                recv_sem=recv.at[d - 1],
                device_id=peer(d),
                device_id_type=MESH,
            )
        )
        copies[-1].start()
    return copies


def sinkhorn_kernel(
    z_ref, stu_ref, tea_ref,
    wide, row_own, row_x, row_mid, row_z, col_own, col_in,
    xs, xr, zs, zr, ss, sr,
):
    barrier = pltpu.get_barrier_semaphore()
    for peer, count in ((peers_x, 4), (peers_z, 4), (peers_s, 8)):
        for d in range(1, count):
            pl.semaphore_signal(barrier, inc=1, device_id=peer(d), device_id_type=MESH)
    pl.semaphore_wait(barrier, 13)
    tokens = z_ref.shape[0] * 8
    marginal = -math.log2(tokens)

    tea_ref[...] = jnp.zeros_like(tea_ref)
    for sweep in range(ITERS):
        def put_row(b, high, total):
            row_own[sweep, 0, pl.ds(b, 1), :] = high
            row_own[sweep, 1, pl.ds(b, 1), :] = total

        row_stats(z_ref, tea_ref, put_row)
        copies = exchange(row_own.at[sweep], row_x.at[sweep], xs.at[sweep], xr.at[sweep], peers_x, 4)
        for copy in copies:
            copy.wait()
        high, total = merge(
            [(row_own[sweep, 0], row_own[sweep, 1])]
            + [(row_x[sweep, d, 0], row_x[sweep, d, 1]) for d in range(3)]
        )
        row_mid[sweep, 0] = high
        row_mid[sweep, 1] = total
        copies = exchange(row_mid.at[sweep], row_z.at[sweep], zs.at[sweep], zr.at[sweep], peers_z, 4)
        for copy in copies:
            copy.wait()
        high, total = merge(
            [(row_mid[sweep, 0], row_mid[sweep, 1])]
            + [(row_z[sweep, d, 0], row_z[sweep, d, 1]) for d in range(3)]
        )
        stu_ref[...] = marginal - (high + jnp.log(total) * log2e)
        spread_rows(stu_ref, wide)

        def put_col(c, high, total):
            col_own[sweep, 0:1, c * LANES:(c + 1) * LANES] = high
            col_own[sweep, 1:2, c * LANES:(c + 1) * LANES] = total

        col_stats(z_ref, wide, put_col)
        copies = exchange(col_own.at[sweep], col_in.at[sweep], ss.at[sweep], sr.at[sweep], peers_s, 8)
        for copy in copies:
            copy.wait()
        high, total = merge(
            [(col_own[sweep, 0:1, :], col_own[sweep, 1:2, :])]
            + [(col_in[sweep, d, 0:1, :], col_in[sweep, d, 1:2, :]) for d in range(7)]
        )
        tea_ref[...] = marginal - (high + jnp.log(total) * log2e)


def sinkhorn(z):
    rows, cols = z.shape
    lines = rows // LANES
    dma = pltpu.SemaphoreType.DMA
    return pl.pallas_call(
        sinkhorn_kernel,
        out_shape=(
            jax.ShapeDtypeStruct((lines, LANES), jnp.float32),
            jax.ShapeDtypeStruct((1, cols), jnp.float32),
        ),
        in_specs=[pl.BlockSpec(memory_space=pltpu.VMEM)],
        out_specs=(pl.BlockSpec(memory_space=pltpu.VMEM),) * 2,
        scratch_shapes=[
            pltpu.VMEM((rows, LANES), jnp.float32),
            pltpu.VMEM((ITERS, 2, lines, LANES), jnp.float32),
            pltpu.VMEM((ITERS, 3, 2, lines, LANES), jnp.float32),
            pltpu.VMEM((ITERS, 2, lines, LANES), jnp.float32),
            pltpu.VMEM((ITERS, 3, 2, lines, LANES), jnp.float32),
            pltpu.VMEM((ITERS, 2, cols), jnp.float32),
            pltpu.VMEM((ITERS, 7, 2, cols), jnp.float32),
            dma((ITERS, 3)), dma((ITERS, 3)),
            dma((ITERS, 3)), dma((ITERS, 3)),
            dma((ITERS, 7)), dma((ITERS, 7)),
        ],
        compiler_params=pltpu.CompilerParams(
            collective_id=0, has_side_effects=True, vmem_limit_bytes=40 * 2**20
        ),
    )(z)


def squares(rows):
    return jnp.sum(jnp.square(rows.astype(jnp.float32)), axis=1)


def local(student, teacher, band_start):
    stu_rows = student.shape[0]
    tea_rows = teacher.shape[0]
    token_total = stu_rows * lax.axis_size("stu")
    first_stu = lax.axis_index("stu") * stu_rows
    first_tea = lax.axis_index("tea") * tea_rows
    stu_block = (first_stu + jnp.arange(stu_rows, dtype=jnp.int32)) // BLK
    tea_block = (first_tea + jnp.arange(tea_rows, dtype=jnp.int32)) // BLK
    matches = stu_block[:, None] == jnp.arange(band_start.shape[0], dtype=jnp.int32)[None, :]
    lowest = jnp.sum(jnp.where(matches, band_start[None, :], 0), axis=1)
    listed = (tea_block[None, :] >= lowest[:, None]) & (tea_block[None, :] < lowest[:, None] + W)
    student_full = lax.all_gather(student, "tea", axis=1, tiled=True)
    teacher_full = lax.all_gather(teacher, "stu", axis=1, tiled=True)
    inner = lax.dot_general(
        student_full, teacher_full, (((1,), (1,)), ((), ())), preferred_element_type=jnp.float32
    )
    cost = (squares(student_full)[:, None] + squares(teacher_full)[None, :] - 2.0 * inner) / D
    z = jnp.where(listed, -kappa * cost, unlisted)
    stu2, tea2 = sinkhorn(z)
    stu2 = stu2.reshape(stu_rows)
    tea2 = tea2.reshape(tea_rows)
    scaled = jnp.exp2(z + (stu2 + math.log2(token_total))[:, None] + tea2[None, :])
    loss = lax.psum(jnp.sum(scaled * z), ("stu", "tea")) * (-1.0 / (kappa * token_total))
    weights = scaled.astype(jnp.bfloat16)
    row_mass = jnp.sum(weights.astype(jnp.float32), axis=1)
    pulled = jnp.dot(weights, teacher_full, preferred_element_type=jnp.float32)
    partial_terms = row_mass[:, None] * student_full.astype(jnp.float32) - pulled
    grad_student = lax.psum_scatter(partial_terms, "tea", scatter_dimension=1, tiled=True)
    return (grad_student, stu2 / kappa, tea2 / kappa, loss)


def solution(mesh):
    placed = (P("stu", "tea"), P("tea", "stu"), P())
    return jax.shard_map(
        local,
        mesh=mesh,
        in_specs=placed,
        out_specs=(P("stu", "tea"), P("stu"), P("tea"), P()),
        check_vma=False,
    )
```

```python
import functools
import math

import jax
import jax.numpy as jnp
from jax import lax
from jax.experimental import pallas as pl
from jax.experimental.pallas import tpu as pltpu
from jax.sharding import PartitionSpec as P

D = 2048
BLK = 512
W = 4
ITERS = 3
LANES = 128
ROWS = 2048
COLS = 1024
HALF = ROWS // 2
QUARTER = ROWS // 4
TILES = COLS // LANES
LINES = ROWS // LANES
TOKENS = 16384

epsilon = 0.02
kappa = math.log2(math.e) / epsilon
log2e = math.log2(math.e)
log2_tokens = math.log2(TOKENS)
unlisted = -1e30
MESH = pl.DeviceIdType.MESH
f32 = jnp.float32
bf16 = jnp.bfloat16


def aligned(start, size):
    return pl.ds(pl.multiple_of(start, size), size)


def diagonal():
    rows = lax.broadcasted_iota(jnp.int32, (LANES, LANES), 0)
    cols = lax.broadcasted_iota(jnp.int32, (LANES, LANES), 1)
    return rows == cols


def to_lanes(column):
    return jnp.sum(jnp.where(diagonal(), column, 0.0), axis=0, keepdims=True)


def to_sublanes(row):
    return jnp.sum(jnp.where(diagonal(), row, 0.0), axis=1, keepdims=True)


def total_of(parts):
    return functools.reduce(lambda a, b: a + b, parts)


def merge(parts):
    highest = functools.reduce(jnp.maximum, [m for m, _ in parts])
    return highest, total_of([s * jnp.exp2(m - highest) for m, s in parts])


class Place:
    def __init__(self):
        self.s = lax.axis_index("stu")
        self.t = lax.axis_index("tea")
        self.y = lax.div(self.s, 2)
        self.core = lax.rem(self.s, 2)
        self.z = lax.div(self.t, 4)
        self.x = lax.rem(self.t, 4)

    def tea(self, dz, dx):
        return lax.rem(self.z + dz, 4) * 4 + lax.rem(self.x + dx, 4)

    def stu(self, dy, dc=0):
        return lax.rem(self.y + dy, 4) * 2 + lax.rem(self.core + dc, 2)

    def at_x(self, d):
        return (self.s, self.tea(0, d))

    def at_z(self, d):
        return (self.s, self.tea(d, 0))

    def at_y(self, d):
        return (self.stu(d), self.t)

    def sibling(self):
        return (self.stu(0, 1), self.t)

    def at_s(self, d):
        return (lax.rem(self.s + d, 8), self.t)


class Wire:
    def __init__(self, send, recv):
        self.send, self.recv, self.used, self.open = send, recv, 0, []

    def start(self, src, dst, device):
        copy = pltpu.make_async_remote_copy(
            src_ref=src, dst_ref=dst,
            send_sem=self.send.at[self.used], recv_sem=self.recv.at[self.used],
            device_id=device, device_id_type=MESH,
        )
        self.used += 1
        copy.start()
        self.open.append(copy)
        return copy

    def drain(self):
        for copy in self.open:
            copy.wait_send()
        self.open = []


WIRES = 200


def gather(me, wire, stu_in, tea_in, S, T, cost_chunk):
    A, B = pl.ds(0, HALF), pl.ds(HALF, HALF)
    quarter = [pl.ds(i * QUARTER, QUARTER) for i in range(4)]

    def piece(dz, dx, rows):
        return S.at[me.tea(dz, dx), rows]

    def push(dz, dx, rows, device):
        return wire.start(piece(dz, dx, rows), piece(dz, dx, rows), device)

    S[me.t] = stu_in[...]
    T[me.s] = tea_in[...]
    up, down = 1, 3
    ax = {up: push(0, 0, A, me.at_x(up)), down: push(0, 0, A, me.at_x(down))}
    bz = {up: push(0, 0, B, me.at_z(up)), down: push(0, 0, B, me.at_z(down))}
    az, bx = {}, {}

    def turn_a(dx):
        for way in (up, down):
            az[dx, way] = push(0, dx, A, me.at_z(way))

    def turn_b(dz):
        for way in (up, down):
            bx[dz, way] = push(dz, 0, B, me.at_x(way))

    turn_a(0)
    turn_b(0)
    t_half = [pl.ds(0, COLS // 2), pl.ds(COLS // 2, COLS // 2)]

    def t_push(dy, dc, rows, device):
        ref = T.at[me.stu(dy, dc), rows]
        return wire.start(ref, ref, device)

    everything = pl.ds(0, COLS)
    ty = {way: t_push(0, 0, everything, me.at_y(way)) for way in (up, down)}
    tc = {0: [t_push(0, 0, everything, me.sibling())]}

    ax_far, bz_far = [], []
    for way, back, keep in ((up, down, 0), (down, up, 1)):
        ax[way].wait_recv()
        ax_far.append(push(0, back, quarter[keep], me.at_x(way)))
        turn_a(back)
        bz[way].wait_recv()
        bz_far.append(push(back, 0, quarter[2 + keep], me.at_z(way)))
        turn_b(back)
    ty_far = []
    for way, back, keep in ((up, down, 0), (down, up, 1)):
        ty[way].wait_recv()
        ty_far.append(t_push(back, 0, t_half[keep], me.at_y(way)))
        tc[back] = [t_push(back, 0, everything, me.sibling())]
    for copy in ax_far:
        copy.wait_recv()
    turn_a(2)
    for copy in bz_far:
        copy.wait_recv()
    turn_b(2)
    tc[2] = []
    for keep, copy in enumerate(ty_far):
        copy.wait_recv()
        tc[2].append(t_push(2, 0, t_half[keep], me.sibling()))

    az_far, bx_far = [], []
    for d in (0, down, up, 2):
        for way, back, keep in ((up, down, 0), (down, up, 1)):
            az[d, way].wait_recv()
            az_far.append(push(back, d, quarter[keep], me.at_z(way)))
            bx[d, way].wait_recv()
            copy = push(d, back, quarter[2 + keep], me.at_x(way))
            bx_far.append((d, copy))
    for dy in (0, down, up, 2):
        for copy in tc[dy]:
            copy.wait_recv()

    def wait_bx(d):
        for at, copy in bx_far:
            if at == d:
                copy.wait_recv()

    for number, dz in enumerate((0, down, up, 2)):
        wait_bx(dz)
        if dz == 2:
            for copy in az_far:
                copy.wait_recv()
        row = lax.rem(me.z + dz, 4)
        cost_chunk(2 * row, number == 0)
        cost_chunk(2 * row + 1, False)


def cost_chunk_of(S, T, z, xsq, ysq):
    def cost_chunk(q, first):
        def rows_block(r, carry):
            rows = aligned(r * 256, 256)
            low, high = S[2 * q, rows, :], S[2 * q + 1, rows, :]
            prod = lax.dot_general(
                jnp.concatenate([low, high], axis=1), T[q],
                (((1,), (1,)), ((), ())), preferred_element_type=f32,
            )
            squared = jnp.square(low.astype(f32)) + jnp.square(high.astype(f32))
            for c in range(TILES):
                tile = prod[:, c * LANES:(c + 1) * LANES]
                z[c, rows, :] = tile if first else z[c, rows, :] + tile
            xsq[rows, :] = squared if first else xsq[rows, :] + squared
            return carry

        lax.fori_loop(0, ROWS // 256, rows_block, 0)

        def cols_block(r, carry):
            rows = aligned(r * LANES, LANES)
            low, high = T[q, rows, :LANES], T[q, rows, LANES:]
            squared = jnp.square(low.astype(f32)) + jnp.square(high.astype(f32))
            ysq[rows, :] = squared if first else ysq[rows, :] + squared
            return carry

        lax.fori_loop(0, TILES, cols_block, 0)

    return cost_chunk


def finish_cost(me, band, z, xsq, ysq, ysq_row):
    for c in range(TILES):
        column = jnp.sum(ysq[c * LANES:(c + 1) * LANES, :], axis=1, keepdims=True)
        ysq_row[:, c * LANES:(c + 1) * LANES] = to_lanes(column)
    scale = kappa / D

    def block(b, carry):
        rows = aligned(b * LANES, LANES)
        total = jnp.broadcast_to(jnp.sum(xsq[rows, :], axis=1, keepdims=True), (LANES, LANES))
        xsq[rows, :] = total
        lowest = jnp.full((LANES, LANES), band[me.s * 4 + lax.div(b, BLK // LANES)], jnp.int32)
        for side in range(2):
            at = jnp.full((LANES, LANES), me.t * 2 + side, jnp.int32)
            listed = (at >= lowest) & (at < lowest + W)
            for c in range(side * 4, side * 4 + 4):
                value = (2.0 * z[c, rows, :] - total - ysq_row[:, c * LANES:(c + 1) * LANES]) * scale
                z[c, rows, :] = jnp.where(listed, value, unlisted)
        return carry

    lax.fori_loop(0, LINES, block, 0)


def row_stats(z, tea, put):
    def block(b, carry):
        highs, sums = [], []
        for part in range(4):
            rows = aligned(b * LANES + part * 32, 32)
            scores = [
                z[c, rows, :] + tea[:, c * LANES:(c + 1) * LANES] for c in range(TILES)
            ]
            high = jnp.max(functools.reduce(jnp.maximum, scores), axis=1, keepdims=True)
            highs.append(high)
            sums.append(
                jnp.sum(total_of([jnp.exp2(v - high) for v in scores]), axis=1, keepdims=True)
            )
        put(
            b,
            to_lanes(jnp.concatenate(highs, axis=0)),
            to_lanes(jnp.concatenate(sums, axis=0)),
        )
        return carry

    lax.fori_loop(0, LINES, block, 0)


def spread_rows(compact, wide):
    def block(b, carry):
        column = to_sublanes(compact[pl.ds(b, 1), :])
        wide[aligned(b * LANES, LANES), :] = jnp.broadcast_to(column, (LANES, LANES))
        return carry

    lax.fori_loop(0, LINES, block, 0)


def col_stats(z, wide, put):
    def block(b, carry):
        rows = aligned(b * LANES, LANES)
        pot = wide[rows, :]
        out = []
        for c in range(TILES):
            high, total = carry[c]
            scores = (z[c, rows, :] + pot).reshape(LANES // 8, 8, LANES)
            new = jnp.maximum(high, jnp.max(scores, axis=0))
            total = total * jnp.exp2(high - new) + jnp.sum(jnp.exp2(scores - new[None]), axis=0)
            out.append((new, total))
        return tuple(out)

    start = tuple(
        (jnp.full((8, LANES), unlisted, f32), jnp.zeros((8, LANES), f32)) for _ in range(TILES)
    )
    done = lax.fori_loop(0, LINES, block, start)
    for c, (high, total) in enumerate(done):
        top = jnp.max(high, axis=0, keepdims=True)
        put(c, top, jnp.sum(total * jnp.exp2(high - top), axis=0, keepdims=True))


def swap(wire, slots, index, count, peer):
    copies = [wire.start(slots.at[index], slots.at[index], peer(d)) for d in range(1, count)]
    for copy in copies:
        copy.wait_recv()


def sweeps(me, wire, z, wide, stu, tea, row_x, row_z, col_s):
    tea[...] = jnp.zeros_like(tea)
    for sweep in range(ITERS):
        rx, rz, cs = row_x.at[sweep], row_z.at[sweep], col_s.at[sweep]

        def put_row(b, high, total):
            rx[me.x, 0, pl.ds(b, 1), :] = high
            rx[me.x, 1, pl.ds(b, 1), :] = total

        row_stats(z, tea, put_row)
        swap(wire, rx, me.x, 4, me.at_x)
        high, total = merge([(rx[i, 0], rx[i, 1]) for i in range(4)])
        rz[me.z, 0] = high
        rz[me.z, 1] = total
        swap(wire, rz, me.z, 4, me.at_z)
        high, total = merge([(rz[i, 0], rz[i, 1]) for i in range(4)])
        stu[...] = -log2_tokens - (high + jnp.log(total) * log2e)
        spread_rows(stu, wide)

        def put_col(c, high, total):
            cs[me.s, 0:1, c * LANES:(c + 1) * LANES] = high
            cs[me.s, 1:2, c * LANES:(c + 1) * LANES] = total

        col_stats(z, wide, put_col)
        swap(wire, cs, me.s, 8, me.at_s)
        high, total = merge([(cs[i, 0:1, :], cs[i, 1:2, :]) for i in range(8)])
        tea[...] = -log2_tokens - (high + jnp.log(total) * log2e)


def make_plan(me, z, wide, tea, xsq, ysq_row, w, sum_x):
    def block(b, loss):
        gammas, betas = [], []
        for part in range(4):
            rows = aligned(b * LANES + part * 32, 32)
            pot = wide[rows, :] + log2_tokens
            mass, pull = [], []
            for c in range(TILES):
                cols = slice(c * LANES, (c + 1) * LANES)
                tile = z[c, rows, :]
                scaled = jnp.exp2(tile + pot + tea[:, cols])
                loss = loss + total_of([(scaled * tile)[8 * i:8 * i + 8] for i in range(4)])
                rounded = scaled.astype(bf16)
                w[rows, cols] = rounded
                rounded = rounded.astype(f32)
                mass.append(rounded)
                pull.append(rounded * (ysq_row[:, cols] + (D / kappa) * tile))
            mass = jnp.sum(total_of(mass), axis=1, keepdims=True)
            pull = jnp.sum(total_of(pull), axis=1, keepdims=True)
            own = xsq[rows, 0:1]
            usable = own > 1e-20
            gamma = jnp.where(usable, 0.5 * (mass + pull / jnp.where(usable, own, 1.0)), 0.0)
            gammas.append(gamma)
            betas.append(mass - gamma)
        wide[aligned(b * LANES, LANES), :] = jnp.broadcast_to(
            jnp.concatenate(gammas, axis=0), (LANES, LANES)
        )
        sum_x[me.x, pl.ds(b, 1), :] = to_lanes(jnp.concatenate(betas, axis=0))
        return loss

    loss = lax.fori_loop(0, LINES, block, jnp.zeros((8, LANES), f32))
    sum_x[me.x, LINES:LINES + 8, :] = loss


def pull_chunk_of(S, T, w, wide, G):
    def pull_chunk(q, half):
        def rows_block(r, carry):
            rows = aligned(half * HALF + r * 256, 256)
            prod = jnp.dot(w[rows, :], T[q], preferred_element_type=f32)
            gamma = wide[rows, :]
            for side in range(2):
                own = S[2 * q + side, rows, :].astype(f32)
                G[half, 2 * q + side, aligned(r * 256, 256), :] = (
                    gamma * own - prod[:, side * LANES:(side + 1) * LANES]
                )
            return carry

        lax.fori_loop(0, HALF // 256, rows_block, 0)

    return pull_chunk


def reduce_half(me, wire, half, G, out, near_in, far_in, last_near, last_far, pull, spot, line, cross):
    up, down = 1, 3
    front, back = pl.ds(0, QUARTER), pl.ds(QUARTER, QUARTER)
    packed, sent_near, sent_far, last_packed = out

    def add(dst, terms):
        def block(r, carry):
            rows = aligned(r * 256, 256)
            dst[rows, :] = total_of([term[rows, :].astype(f32) for term in terms]).astype(dst.dtype)
            return carry

        lax.fori_loop(0, dst.shape[0] // 256, block, 0)

    def value(t):
        return G.at[half, t]

    pull(2)
    far = []
    for j in range(4):
        add(sent_far.at[j], [value(spot(2, j))])
        far.append((
            wire.start(sent_far.at[j, front], far_in.at[j, 0], line(up)),
            wire.start(sent_far.at[j, back], far_in.at[j, 1], line(down)),
        ))
    yield
    pull(up)
    pull(down)
    near = []
    for j in range(4):
        for way, keep in ((up, 0), (down, 1)):
            far[j][keep].wait_recv()
            chained, direct = (front, back) if keep == 0 else (back, front)
            mine = value(spot(way, j))
            add(sent_near.at[keep, j, chained], [mine.at[chained], far_in.at[j, keep]])
            add(sent_near.at[keep, j, direct], [mine.at[direct]])
            near.append(wire.start(sent_near.at[keep, j], near_in.at[keep, j], line(way)))
    yield
    pull(0)
    for copy in near:
        copy.wait_recv()
    for j in range(4):
        mine = value(spot(0, j))
        add(mine, [mine, near_in.at[0, j], near_in.at[1, j]])
    yield
    here = lambda d: value(spot(0, cross[1](d)))
    add(last_packed.at[2], [here(2)])
    far = (
        wire.start(last_packed.at[2, front], last_far.at[0], cross[0](up)),
        wire.start(last_packed.at[2, back], last_far.at[1], cross[0](down)),
    )
    yield
    near = []
    for way, keep in ((up, 0), (down, 1)):
        far[keep].wait_recv()
        chained, direct = (front, back) if keep == 0 else (back, front)
        mine = here(way)
        add(last_packed.at[keep, chained], [mine.at[chained], last_far.at[keep]])
        add(last_packed.at[keep, direct], [mine.at[direct]])
        near.append(wire.start(last_packed.at[keep], last_near.at[keep], cross[0](way)))
    yield
    for copy in near:
        copy.wait_recv()
    mine = here(0)
    add(mine, [mine, last_near.at[0], last_near.at[1]])
    yield


def kernel(
    band, stu_in, tea_in, grad, stu, tea, loss,
    S, T, z, z_more, w, wide, xsq, ysq, ysq_row,
    row_x, row_z, col_s, sum_x, sum_z, sum_s, shares,
    sent_near, sent_far, last_packed, near_in, far_in, last_near, last_far,
    send, recv,
):
    me = Place()
    barrier = pltpu.get_barrier_semaphore()
    for peer, count in ((me.at_x, 4), (me.at_z, 4), (me.at_s, 8)):
        for d in range(1, count):
            pl.semaphore_signal(barrier, inc=1, device_id=peer(d), device_id_type=MESH)
    pl.semaphore_wait(barrier, 13)
    wire = Wire(send, recv)
    gather(me, wire, stu_in, tea_in, S, T, cost_chunk_of(S, T, z, xsq, ysq))
    finish_cost(me, band, z, xsq, ysq, ysq_row)
    sweeps(me, wire, z, wide, stu, tea, row_x, row_z, col_s)
    make_plan(me, z, wide, tea, xsq, ysq_row, w, sum_x)
    sums = [wire.start(sum_x.at[me.x], sum_x.at[me.x], me.at_x(d)) for d in range(1, 4)]

    pull_chunk = pull_chunk_of(S, T, w, wide, z_more)

    def pull_a(dz):
        row = lax.rem(me.z + dz, 4)
        pull_chunk(2 * row, 0)
        pull_chunk(2 * row + 1, 0)

    pair = lax.div(me.x, 2)

    def pull_b(dx):
        if dx in (2, 0):
            side = 1 - pair if dx == 2 else pair
            for row in range(4):
                pull_chunk(2 * row + side, 1)

    def pull_b_steps(dx):
        if dx == 2:
            pull_b(2)
        elif dx == 1:
            pull_b(0)

    def buffers(half):
        return (None, sent_near.at[half], sent_far.at[half], last_packed.at[half])

    first = reduce_half(
        me, wire, 0, z_more, buffers(0), near_in.at[0], far_in.at[0], last_near.at[0], last_far.at[0],
        pull_a, lambda i, j: lax.rem(me.z + i, 4) * 4 + j, me.at_z,
        (me.at_x, lambda d: lax.rem(me.x + d, 4)),
    )
    second = reduce_half(
        me, wire, 1, z_more, buffers(1), near_in.at[1], far_in.at[1], last_near.at[1], last_far.at[1],
        pull_b_steps, lambda i, j: j * 4 + lax.rem(me.x + i, 4), me.at_x,
        (me.at_z, lambda d: lax.rem(me.z + d, 4)),
    )
    for step in range(6):
        next(first)
        next(second)
        if step == 0:
            for copy in sums:
                copy.wait_recv()
            sum_z[me.z] = total_of([sum_x[i] for i in range(4)])
            sums = [wire.start(sum_z.at[me.z], sum_z.at[me.z], me.at_z(d)) for d in range(1, 4)]
        if step == 1:
            for copy in sums:
                copy.wait_recv()
            summed = total_of([sum_z[i] for i in range(4)])
            stu[...] = stu[...] / kappa
            tea[...] = tea[...] / kappa
            sum_s[me.s] = summed[LINES:, :]
            shares[...] = summed[:LINES, :]
            sums = [wire.start(sum_s.at[me.s], sum_s.at[me.s], me.at_s(d)) for d in range(1, 8)]
            spread_rows(shares, xsq)
        if step == 2:
            for copy in sums:
                copy.wait_recv()
            loss[...] = total_of([sum_s[i] for i in range(8)])
    for half in range(2):
        def block(r, carry):
            here = aligned(r * 256, 256)
            rows = aligned(half * HALF + r * 256, 256)
            grad[rows, :] = xsq[rows, :] * S[me.t, rows, :].astype(f32) + z_more[half, me.t, here, :]
            return carry

        lax.fori_loop(0, HALF // 256, block, 0)
    wire.drain()


def one_device(band_start, student, teacher):
    dma = pltpu.SemaphoreType.DMA
    vmem = pl.BlockSpec(memory_space=pltpu.VMEM)
    scratch = [
        pltpu.VMEM((16, ROWS, LANES), bf16),
        pltpu.VMEM((8, COLS, 256), bf16),
        pltpu.VMEM((TILES, ROWS, LANES), f32),
        pltpu.VMEM((2, 16, HALF, LANES), f32),
        pltpu.VMEM((ROWS, COLS), bf16),
        pltpu.VMEM((ROWS, LANES), f32),
        pltpu.VMEM((ROWS, LANES), f32),
        pltpu.VMEM((COLS, LANES), f32),
        pltpu.VMEM((1, COLS), f32),
        pltpu.VMEM((ITERS, 4, 2, LINES, LANES), f32),
        pltpu.VMEM((ITERS, 4, 2, LINES, LANES), f32),
        pltpu.VMEM((ITERS, 8, 2, COLS), f32),
        pltpu.VMEM((4, LINES + 8, LANES), f32),
        pltpu.VMEM((4, LINES + 8, LANES), f32),
        pltpu.VMEM((8, 8, LANES), f32),
        pltpu.VMEM((LINES, LANES), f32),
        pltpu.VMEM((2, 2, 4, HALF, LANES), bf16),
        pltpu.VMEM((2, 4, HALF, LANES), bf16),
        pltpu.VMEM((2, 3, HALF, LANES), bf16),
        pltpu.VMEM((2, 2, 4, HALF, LANES), bf16),
        pltpu.VMEM((2, 4, 2, QUARTER, LANES), bf16),
        pltpu.VMEM((2, 2, HALF, LANES), bf16),
        pltpu.VMEM((2, 2, QUARTER, LANES), bf16),
        dma((WIRES,)),
        dma((WIRES,)),
    ]
    return pl.pallas_call(
        kernel,
        out_shape=(
            jax.ShapeDtypeStruct((ROWS, LANES), f32),
            jax.ShapeDtypeStruct((LINES, LANES), f32),
            jax.ShapeDtypeStruct((1, COLS), f32),
            jax.ShapeDtypeStruct((8, LANES), f32),
        ),
        in_specs=[pl.BlockSpec(memory_space=pltpu.SMEM), vmem, vmem],
        out_specs=(vmem,) * 4,
        scratch_shapes=scratch,
        compiler_params=pltpu.CompilerParams(
            collective_id=0, has_side_effects=True, vmem_limit_bytes=62 * 2**20
        ),
    )(band_start, student, teacher)


def local(student, teacher, band_start):
    grad, stu, tea, loss = one_device(band_start, student, teacher)
    loss = jnp.sum(loss) * (-1.0 / (kappa * TOKENS))
    return (grad, stu.reshape(ROWS), tea.reshape(COLS), loss)


def solution(mesh):
    placed = (P("stu", "tea"), P("tea", "stu"), P())
    return jax.shard_map(
        local,
        mesh=mesh,
        in_specs=placed,
        out_specs=(P("stu", "tea"), P("stu"), P("tea"), P()),
        check_vma=False,
    )
```

```python
import functools
import math

import jax
import jax.numpy as jnp
from jax import lax
from jax.experimental import pallas as pl
from jax.experimental.pallas import tpu as pltpu
from jax.sharding import PartitionSpec as P

D = 2048
BLK = 512
W = 4
ITERS = 3
LANES = 128
OWNED = 2048
ROWS = 1024
COLS = 2048
PIECE = 1024
TILES = COLS // LANES
LINES = ROWS // LANES
TOKENS = 16384
GA, GB = 768, 256
RHALF = ROWS // 2
WIRES = 240
UP, DOWN = 1, 3

epsilon = 0.02
kappa = math.log2(math.e) / epsilon
log2e = math.log2(math.e)
log2_tokens = math.log2(TOKENS)
unlisted = -1e30
MESH = pl.DeviceIdType.MESH
f32 = jnp.float32
bf16 = jnp.bfloat16


def aligned(start, size):
    return pl.ds(pl.multiple_of(start, size), size)


def diagonal():
    rows = lax.broadcasted_iota(jnp.int32, (LANES, LANES), 0)
    cols = lax.broadcasted_iota(jnp.int32, (LANES, LANES), 1)
    return rows == cols


def to_lanes(column):
    return jnp.sum(jnp.where(diagonal(), column, 0.0), axis=0, keepdims=True)


def to_sublanes(row):
    return jnp.sum(jnp.where(diagonal(), row, 0.0), axis=1, keepdims=True)


def total_of(parts):
    return functools.reduce(lambda a, b: a + b, parts)


def merge(parts):
    highest = functools.reduce(jnp.maximum, parts)
    return highest + jnp.log(total_of([jnp.exp2(p - highest) for p in parts])) * log2e


class Place:
    def __init__(self):
        self.s = lax.axis_index("stu")
        self.t = lax.axis_index("tea")
        self.y = lax.div(self.s, 2)
        self.core = lax.rem(self.s, 2)
        self.z = lax.div(self.t, 4)
        self.x = lax.rem(self.t, 4)
        self.h = lax.rem(self.x, 2)
        self.l = lax.div(self.x, 2)
        self.row_slot = 2 * self.z + self.l
        self.col_slot = 2 * self.s + self.h

    def zi(self, dz):
        return lax.rem(self.z + dz, 4)

    def xi(self, dx):
        return lax.rem(self.x + dx, 4)

    def tea(self, dz, dx):
        return self.zi(dz) * 4 + self.xi(dx)

    def stu(self, dy):
        return lax.rem(self.y + dy, 4) * 2 + self.core

    def at_x(self, d):
        return (self.s, self.tea(0, d))

    def at_z(self, d):
        return (self.s, self.tea(d, 0))

    def at_y(self, d):
        return (self.stu(d), self.t)

    def sibling(self):
        return (self.y * 2 + 1 - self.core, self.t)

    def partner(self):
        return (self.s, self.z * 4 + self.l * 2 + 1 - self.h)

    def outer(self):
        return (self.s, self.z * 4 + lax.rem(self.x + 3 + 2 * self.h, 4))

    def at_row(self, d):
        k = lax.rem(self.row_slot + d, 8)
        return (self.s, lax.div(k, 2) * 4 + lax.rem(k, 2) * 2 + self.h)

    def at_col(self, d):
        k = lax.rem(self.col_slot + d, 16)
        return (lax.div(k, 2), self.z * 4 + self.l * 2 + lax.rem(k, 2))


class Wire:
    def __init__(self, send, recv):
        self.send, self.recv, self.used, self.open = send, recv, 0, []

    def start(self, src, dst, device):
        copy = pltpu.make_async_remote_copy(
            src_ref=src, dst_ref=dst,
            send_sem=self.send.at[self.used], recv_sem=self.recv.at[self.used],
            device_id=device, device_id_type=MESH,
        )
        self.used += 1
        copy.start()
        self.open.append(copy)
        return copy

    def drain(self):
        for copy in self.open:
            copy.wait_send()
        self.open = []


WAYS = ((UP, DOWN, 0), (DOWN, UP, 1))


def gather(me, wire, stu_in, tea_in, S, T, X, relay_a, relay_b, cost):
    A, B = pl.ds(0, GA), pl.ds(GA, GB)
    a_part = [pl.ds(0, GA // 2), pl.ds(GA // 2, GA // 2)]
    b_part = [pl.ds(GA, GB // 2), pl.ds(GA + GB // 2, GB // 2)]
    x_part = [pl.ds(0, GB // 2), pl.ds(GB // 2, GB // 2)]
    t_part = [pl.ds(0, PIECE // 2), pl.ds(PIECE // 2, PIECE // 2)]
    mine = pl.multiple_of(me.h * ROWS, ROWS)
    others = pl.multiple_of((1 - me.h) * ROWS, ROWS)

    def push(ref, device):
        return wire.start(ref, ref, device)

    def piece(dz, dx, rows):
        return S.at[me.tea(dz, dx), rows]

    def t_push(dy, e, rows, device):
        return push(T.at[me.stu(dy), e, rows], device)

    own, other = me.h, 1 - me.h
    whole = pl.ds(0, PIECE)
    T[me.s, own] = tea_in[...]
    tp = t_push(0, own, whole, me.partner())
    ty = {(0, way): t_push(0, own, whole, me.at_y(way)) for way in (UP, DOWN)}
    tc = {0: [t_push(0, own, whole, me.sibling())], 1: []}
    S[me.t] = stu_in[pl.ds(mine, ROWS), :]
    X[me.z] = stu_in[pl.ds(others + GA, GB), :]
    ax, ar, axf, az, azf = {}, {}, {}, {}, []
    bz, bzf, bx, br, bxf = {}, [], {}, {}, {}
    for way, back, keep in WAYS:
        ar[way] = wire.start(S.at[me.t, a_part[keep]], relay_a.at[keep], me.at_x(way))
        ax[way] = wire.start(stu_in.at[pl.ds(others, GA)], S.at[me.t, A], me.at_x(way))

    def turn_a(dx):
        for way in (UP, DOWN):
            az[dx, way] = push(piece(0, dx, A), me.at_z(way))

    def turn_b(dz):
        for way, back, keep in WAYS:
            bx[dz, way] = wire.start(X.at[me.zi(dz)], piece(dz, 0, B), me.at_x(way))
            br[dz, way] = wire.start(
                piece(dz, 0, b_part[keep]), relay_b.at[me.zi(dz), keep], me.at_x(way)
            )

    turn_a(0)
    for way in (UP, DOWN):
        bz[way] = (push(piece(0, 0, B), me.at_z(way)), push(X.at[me.z], me.at_z(way)))
    turn_b(0)

    for way, back, keep in WAYS:
        ar[way].wait_recv()
        axf[way] = wire.start(relay_a.at[keep], piece(0, back, a_part[keep]), me.at_x(way))
    for way, back, keep in WAYS:
        ax[way].wait_recv()
        turn_a(back)
    for way, back, keep in WAYS:
        for copy in bz[way]:
            copy.wait_recv()
        bzf.append(push(piece(back, 0, b_part[keep]), me.at_z(way)))
        bzf.append(push(X.at[me.zi(back), x_part[keep]], me.at_z(way)))
        turn_b(back)
    tyf = {0: [], 1: []}

    def t_relay(order, e):
        for way, back, keep in WAYS:
            ty[order, way].wait_recv()
            tyf[order].append(t_push(back, e, t_part[keep], me.at_y(way)))
            tc[order].append(t_push(back, e, whole, me.sibling()))

    def t_last(order, e):
        for keep, copy in enumerate(tyf[order]):
            copy.wait_recv()
            tc[order].append(t_push(2, e, t_part[keep], me.sibling()))

    t_relay(0, own)
    tp.wait_recv()
    for way in (UP, DOWN):
        ty[1, way] = t_push(0, other, whole, me.at_y(way))
    tc[1].append(t_push(0, other, whole, me.sibling()))
    for copy in axf.values():
        copy.wait_recv()
    turn_a(2)
    for copy in bzf:
        copy.wait_recv()
    turn_b(2)

    def b_relay(dz):
        bxf[dz] = []
        for way, back, keep in WAYS:
            br[dz, way].wait_recv()
            bxf[dz].append(
                wire.start(relay_b.at[me.zi(dz), keep], piece(dz, back, b_part[keep]), me.at_x(way))
            )

    def a_relay(dx):
        for way, back, keep in WAYS:
            az[dx, way].wait_recv()
            azf.append(push(piece(back, dx, a_part[keep]), me.at_z(way)))

    for d in (0, DOWN, UP):
        b_relay(d)
        a_relay(d)
    t_last(0, own)
    t_relay(1, other)
    b_relay(2)
    a_relay(2)

    def b_here(dz):
        for way in (UP, DOWN):
            bx[dz, way].wait_recv()
        for copy in bxf[dz]:
            copy.wait_recv()

    for copy in tc[0]:
        copy.wait_recv()
    b_here(0)
    cost(me.zi(0), own, True)
    b_here(DOWN)
    cost(me.zi(DOWN), own, False)
    b_here(UP)
    cost(me.zi(UP), own, False)
    t_last(1, other)
    for copy in azf:
        copy.wait_recv()
    b_here(2)
    cost(me.zi(2), own, False)
    for copy in tc[1]:
        copy.wait_recv()
    for number, dz in enumerate((0, DOWN, UP, 2)):
        cost(me.zi(dz), other, number == 0)


def cost_of(S, T, z, xsq, ysq):
    def cost(group, e, first):
        def rows_block(r, carry):
            rows = aligned(r * 256, 256)
            pieces = [S[4 * group + i, rows, :] for i in range(4)]
            prod = total_of([
                lax.dot_general(
                    jnp.concatenate(pieces[2 * i:2 * i + 2], axis=1), T[2 * group + i, e],
                    (((1,), (1,)), ((), ())), preferred_element_type=f32,
                )
                for i in range(2)
            ])
            for c in range(TILES // 2):
                tile = prod[:, c * LANES:(c + 1) * LANES]
                at = e * (TILES // 2) + c
                z[at, rows, :] = tile if first else z[at, rows, :] + tile
            return carry

        lax.fori_loop(0, ROWS // 256, rows_block, 0)

        def cols_block(r, carry):
            rows = aligned(r * LANES, LANES)
            squared = total_of([
                jnp.square(T[2 * group + i, e, rows, side * LANES:(side + 1) * LANES].astype(f32))
                for i in range(2) for side in range(2)
            ])
            ysq[e, rows, :] = squared if first else ysq[e, rows, :] + squared
            return carry

        lax.fori_loop(0, PIECE // LANES, cols_block, 0)

    return cost


def finish_cost(me, band, S, z, xsq, ysq, ysq_row):
    for e in range(2):
        def lines(c, carry):
            column = jnp.sum(ysq[e, aligned(c * LANES, LANES), :], axis=1, keepdims=True)
            ysq_row[pl.ds(e * (TILES // 2) + c, 1), :] = to_lanes(column)
            return carry

        lax.fori_loop(0, TILES // 2, lines, 0)
    scale = kappa / D

    def block(b, carry):
        rows = aligned(b * LANES, LANES)
        squared = total_of([jnp.square(S[i, rows, :].astype(f32)) for i in range(16)])
        total = jnp.broadcast_to(jnp.sum(squared, axis=1, keepdims=True), (LANES, LANES))
        xsq[rows, :] = total
        lowest = band[me.s * 4 + me.h * 2 + lax.div(b, BLK // LANES)]
        lowest = jnp.full((LANES, LANES), lowest, jnp.int32)
        for group in range(TILES // 4):
            at = jnp.full((LANES, LANES), me.row_slot * 4 + group, jnp.int32)
            listed = (at >= lowest) & (at < lowest + W)
            for c in range(group * 4, group * 4 + 4):
                value = (2.0 * z[c, rows, :] - total - ysq_row[c:c + 1, :]) * scale
                z[c, rows, :] = jnp.where(listed, value, unlisted)
        return carry

    lax.fori_loop(0, LINES, block, 0)


def row_stats(z, tea, put):
    def block(b, carry):
        highs, sums = [], []
        for part in range(8):
            rows = aligned(b * LANES + part * 16, 16)
            scores = [z[c, rows, :] + tea[c:c + 1, :] for c in range(TILES)]
            high = jnp.max(functools.reduce(jnp.maximum, scores), axis=1, keepdims=True)
            highs.append(high)
            sums.append(
                jnp.sum(total_of([jnp.exp2(v - high) for v in scores]), axis=1, keepdims=True)
            )
        high = to_lanes(jnp.concatenate(highs, axis=0))
        total = to_lanes(jnp.concatenate(sums, axis=0))
        put(b, high + jnp.log(total) * log2e)
        return carry

    lax.fori_loop(0, LINES, block, 0)


def spread_rows(compact, wide):
    def block(b, carry):
        column = to_sublanes(compact[pl.ds(b, 1), :])
        wide[aligned(b * LANES, LANES), :] = jnp.broadcast_to(column, (LANES, LANES))
        return carry

    lax.fori_loop(0, LINES, block, 0)


def col_stats(z, wide, put):
    def tile(c, carry):
        high = jnp.full((8, LANES), unlisted, f32)
        total = jnp.zeros((8, LANES), f32)
        for b in range(LINES):
            rows = pl.ds(b * LANES, LANES)
            scores = (z[c, rows, :] + wide[rows, :]).reshape(LANES // 8, 8, LANES)
            new = jnp.maximum(high, jnp.max(scores, axis=0))
            total = total * jnp.exp2(high - new) + jnp.sum(jnp.exp2(scores - new[None]), axis=0)
            high = new
        top = jnp.max(high, axis=0, keepdims=True)
        total = jnp.sum(total * jnp.exp2(high - top), axis=0, keepdims=True)
        put(c, top + jnp.log(total) * log2e)
        return carry

    lax.fori_loop(0, TILES, tile, 0)


def tell(wire, slots, index, count, peer):
    return [wire.start(slots.at[index], slots.at[index], peer(d)) for d in range(1, count)]


def swap(wire, slots, index, count, peer):
    for copy in tell(wire, slots, index, count, peer):
        copy.wait_recv()


def sweeps(me, wire, z, wide, stu, tea, row_l, col_l):
    tea[...] = jnp.zeros_like(tea)
    for sweep in range(ITERS):
        rl, cl = row_l.at[sweep], col_l.at[sweep]

        def put_row(b, value):
            rl[me.row_slot, pl.ds(b, 1), :] = value

        row_stats(z, tea, put_row)
        swap(wire, rl, me.row_slot, 8, me.at_row)
        stu[...] = -log2_tokens - merge([rl[i] for i in range(8)])
        spread_rows(stu, wide)

        def put_col(c, value):
            cl[me.col_slot, pl.ds(c, 1), :] = value

        col_stats(z, wide, put_col)
        swap(wire, cl, me.col_slot, 16, me.at_col)
        tea[...] = -log2_tokens - merge([cl[i] for i in range(16)])


def make_plan(me, z, wide, tea, xsq, ysq_row, w, sum_r):
    def block(b, loss):
        gammas, betas = [], []
        for part in range(8):
            rows = aligned(b * LANES + part * 16, 16)
            pot = wide[rows, :] + log2_tokens
            mass, pull = [], []
            for c in range(TILES):
                tile = z[c, rows, :]
                scaled = jnp.exp2(tile + pot + tea[c:c + 1, :])
                loss = loss + total_of([(scaled * tile)[8 * i:8 * i + 8] for i in range(2)])
                rounded = scaled.astype(bf16)
                w[rows, c * LANES:(c + 1) * LANES] = rounded
                rounded = rounded.astype(f32)
                mass.append(rounded)
                pull.append(rounded * (ysq_row[c:c + 1, :] + (D / kappa) * tile))
            mass = jnp.sum(total_of(mass), axis=1, keepdims=True)
            pull = jnp.sum(total_of(pull), axis=1, keepdims=True)
            own = xsq[rows, 0:1]
            usable = own > 1e-20
            gamma = jnp.where(usable, 0.5 * (mass + pull / jnp.where(usable, own, 1.0)), 0.0)
            gammas.append(gamma)
            betas.append(mass - gamma)
        wide[aligned(b * LANES, LANES), :] = jnp.broadcast_to(
            jnp.concatenate(gammas, axis=0), (LANES, LANES)
        )
        sum_r[me.row_slot, pl.ds(b, 1), :] = to_lanes(jnp.concatenate(betas, axis=0))
        return loss

    loss = lax.fori_loop(0, LINES, block, jnp.zeros((8, LANES), f32))
    sum_r[me.row_slot, LINES:LINES + 8, :] = loss


def pull_of(S, T, w, wide, G):
    def pull(q, part):
        def rows_block(r, carry):
            rows = aligned(part * RHALF + r * 256, 256)
            prod = jnp.dot(
                w[rows, :], T[q].reshape(COLS, 2 * LANES), preferred_element_type=f32
            )
            gamma = wide[rows, :]
            for side in range(2):
                own = S[2 * q + side, rows, :].astype(f32)
                G[2 * q + side, rows, :] = gamma * own - prod[:, side * LANES:(side + 1) * LANES]
            return carry

        lax.fori_loop(0, RHALF // 256, rows_block, 0)

    return pull


def add(dst, terms):
    def block(r, carry):
        rows = aligned(r * 256, 256)
        dst[rows, :] = total_of([term[rows, :].astype(f32) for term in terms]).astype(dst.dtype)
        return carry

    lax.fori_loop(0, dst.shape[0] // 256, block, 0)


PARTS = (pl.ds(0, RHALF // 2), pl.ds(RHALF // 2, RHALF // 2))


def reduce_a(me, wire, G, pull, far_out, near_out, far_in, near_in, x_out, x_in, x_relay, x_far):
    def value(t):
        return G.at[t, pl.ds(0, RHALF)]

    def pull_to(dz):
        for k in range(2):
            pull(2 * me.zi(dz) + k, 0)

    pull_to(2)
    far = []
    for j in range(4):
        add(far_out.at[j], [value(me.zi(2) * 4 + j)])
        far.append([
            wire.start(far_out.at[j, PARTS[keep]], far_in.at[j, keep], me.at_z(way))
            for way, back, keep in WAYS
        ])
    yield
    pull_to(UP)
    pull_to(DOWN)
    near = []
    for j in range(4):
        for way, back, keep in WAYS:
            far[j][keep].wait_recv()
            chained, direct = PARTS[keep], PARTS[1 - keep]
            mine = value(me.zi(way) * 4 + j)
            out = near_out.at[keep, j]
            add(out.at[chained], [mine.at[chained], far_in.at[j, keep]])
            add(out.at[direct], [mine.at[direct]])
            near.append(wire.start(out, near_in.at[keep, j], me.at_z(way)))
    yield
    pull_to(0)
    for copy in near:
        copy.wait_recv()
    for j in range(4):
        mine = value(me.z * 4 + j)
        add(mine, [mine, near_in.at[0, j], near_in.at[1, j]])
    add(x_out.at[2], [value(me.tea(0, 2))])
    far = [
        wire.start(x_out.at[2, PARTS[keep]], x_relay.at[keep], me.at_x(way))
        for way, back, keep in WAYS
    ]
    near = []
    for way, back, keep in WAYS:
        add(x_out.at[keep], [value(me.tea(0, way))])
        near.append(wire.start(x_out.at[keep], x_in.at[keep], me.at_x(way)))
    yield
    last = []
    for way, back, keep in WAYS:
        far[keep].wait_recv()
        last.append(wire.start(x_relay.at[keep], x_far.at[PARTS[keep]], me.at_x(way)))
    yield
    for copy in near + last:
        copy.wait_recv()
    yield


def reduce_b(
    me, wire, G, pull, far_out, relay, x_out, x_in, x_far, others,
    z_far_out, z_far_in, z_out, z_in,
):
    order = (2, UP, DOWN, 0)

    def value(t):
        return G.at[t, pl.ds(RHALF, RHALF)]

    far, near, last = {}, {}, {}
    for dz in order:
        pull(2 * me.zi(dz) + 1 - me.l, 1)
        add(far_out.at[me.zi(dz)], [value(me.tea(dz, 2))])
        far[dz] = [
            wire.start(
                far_out.at[me.zi(dz), PARTS[keep]], relay.at[me.zi(dz), keep], me.at_x(way)
            )
            for way, back, keep in WAYS
        ]
    yield
    for dz in order:
        pull(2 * me.zi(dz) + me.l, 1)
        near[dz] = []
        for way, back, keep in WAYS:
            add(x_out.at[keep, me.zi(dz)], [value(me.tea(dz, way))])
            near[dz].append(
                wire.start(x_out.at[keep, me.zi(dz)], x_in.at[keep, me.zi(dz)], me.at_x(way))
            )
        last[dz] = []
        for way, back, keep in WAYS:
            far[dz][keep].wait_recv()
            last[dz].append(
                wire.start(relay.at[me.zi(dz), keep], x_far.at[me.zi(dz), PARTS[keep]], me.at_x(way))
            )
    yield

    def arrived(dz):
        for copy in near[dz] + last[dz]:
            copy.wait_recv()
        mine, other = value(me.tea(dz, 0)), others.at[me.zi(dz)]
        add(mine, [mine, x_far.at[me.zi(dz)]])
        add(other, [x_in.at[0, me.zi(dz)], x_in.at[1, me.zi(dz)]])
        return mine, other

    z_far = {}
    for i, term in enumerate(arrived(2)):
        add(z_far_out.at[i], [term])
        for way, back, keep in WAYS:
            z_far[i, way] = wire.start(
                z_far_out.at[i, PARTS[keep]], z_far_in.at[i, keep], me.at_z(way)
            )
    yield
    z_near = []
    terms = {way: arrived(way) for way in (UP, DOWN)}
    for i in range(2):
        for way, back, keep in WAYS:
            z_far[i, way].wait_recv()
            chained, direct = PARTS[keep], PARTS[1 - keep]
            term, out = terms[way][i], z_out.at[i, keep]
            add(out.at[chained], [term.at[chained], z_far_in.at[i, keep]])
            add(out.at[direct], [term.at[direct]])
            z_near.append(wire.start(out, z_in.at[i, keep], me.at_z(way)))
    yield
    terms = arrived(0)
    for copy in z_near:
        copy.wait_recv()
    for i, term in enumerate(terms):
        add(term, [term, z_in.at[i, 0], z_in.at[i, 1]])
    yield


def kernel(
    band, stu_in, tea_in, grad, stu_out, tea_out, loss,
    S, T, X, relay_a, relay_b, z, w, G, wide, xsq, ysq, ysq_row, stu, tea,
    row_l, col_l, sum_r, sum_c, pair_f, pair_b, others,
    a_far_out, a_near_out, a_far_in, a_near_in, a_x_out, a_x_in, a_x_relay, a_x_far,
    b_far_out, b_relay, b_x_out, b_x_in, b_x_far, b_z_far_out, b_z_far_in, b_z_out, b_z_in,
    send, recv,
):
    me = Place()
    barrier = pltpu.get_barrier_semaphore()
    peers = [me.outer()] + [me.at_row(d) for d in range(1, 8)] + [me.at_col(d) for d in range(1, 16)]
    for peer in peers:
        pl.semaphore_signal(barrier, inc=1, device_id=peer, device_id_type=MESH)
    pl.semaphore_wait(barrier, len(peers))
    wire = Wire(send, recv)
    gather(me, wire, stu_in, tea_in, S, T, X, relay_a, relay_b, cost_of(S, T, z, xsq, ysq))
    finish_cost(me, band, S, z, xsq, ysq, ysq_row)
    sweeps(me, wire, z, wide, stu, tea, row_l, col_l)
    make_plan(me, z, wide, tea, xsq, ysq_row, w, sum_r)
    sums = tell(wire, sum_r, me.row_slot, 8, me.at_row)
    pair_f[me.h] = stu[...] / kappa
    sums.append(wire.start(pair_f.at[me.h], pair_f.at[me.h], me.partner()))
    pull = pull_of(S, T, w, wide, G)
    first = reduce_a(
        me, wire, G, pull, a_far_out, a_near_out, a_far_in, a_near_in,
        a_x_out, a_x_in, a_x_relay, a_x_far,
    )
    second = reduce_b(
        me, wire, G, pull, b_far_out, b_relay, b_x_out, b_x_in, b_x_far, others,
        b_z_far_out, b_z_far_in, b_z_out, b_z_in,
    )
    steps = [first, second] * 3 + [second, first, second, first]
    for number, step in enumerate(steps):
        next(step)
        if number == 1:
            for copy in sums:
                copy.wait_recv()
            summed = total_of([sum_r[i] for i in range(8)])
            sum_c[me.col_slot] = summed[LINES:, :]
            pair_b[me.h] = summed[:LINES, :]
            sums = tell(wire, sum_c, me.col_slot, 16, me.at_col)
            sums.append(wire.start(pair_b.at[me.h], pair_b.at[me.h], me.partner()))
            stu_out[...] = pair_f[...]
            tea_out[...] = tea[aligned(me.h * LINES, LINES), :] / kappa
        if number == 3:
            for copy in sums:
                copy.wait_recv()
            total = total_of([sum_c[i] for i in range(16)])
            total = jnp.sum(jnp.sum(total, axis=0, keepdims=True), axis=1, keepdims=True)
            loss[...] = total * (-1.0 / (kappa * TOKENS))
            spread_rows(pair_b.at[me.h], xsq)
            spread_rows(pair_b.at[1 - me.h], ysq.at[0])
    mine = pl.multiple_of(me.h * ROWS, ROWS)
    other = pl.multiple_of((1 - me.h) * ROWS, ROWS)

    def finish(r, carry):
        rows = aligned(r * 256, 256)
        tail = aligned(RHALF + r * 256, 256)
        grad[aligned(mine + r * 256, 256), :] = (
            xsq[rows, :] * S[me.t, rows, :].astype(f32)
            + G[me.t, rows, :] + a_x_far[rows, :].astype(f32)
        )
        grad[aligned(mine + RHALF + r * 256, 256), :] = (
            xsq[tail, :] * S[me.t, tail, :].astype(f32) + G[me.t, tail, :]
        )
        there = aligned(other + r * 256, 256)
        grad[there, :] = (
            ysq[0, rows, :] * stu_in[there, :].astype(f32)
            + a_x_in[0, rows, :].astype(f32) + a_x_in[1, rows, :].astype(f32)
        )
        there = aligned(other + RHALF + r * 256, 256)
        grad[there, :] = (
            ysq[0, tail, :] * stu_in[there, :].astype(f32) + others[me.z, rows, :]
        )
        return carry

    lax.fori_loop(0, RHALF // 256, finish, 0)
    wire.drain()


def one_device(band_start, student, teacher):
    dma = pltpu.SemaphoreType.DMA
    vmem = pl.BlockSpec(memory_space=pltpu.VMEM)
    half, part = RHALF, RHALF // 2

    def wide_bf16(*lead):
        return pltpu.VMEM((*lead, LANES), bf16)

    def wide_f32(*lead):
        return pltpu.VMEM((*lead, LANES), f32)

    scratch = [
        wide_bf16(16, ROWS),
        pltpu.VMEM((8, 2, PIECE, 2 * LANES), bf16),
        wide_bf16(4, GB),
        wide_bf16(2, GA // 2),
        wide_bf16(4, 2, GB // 2),
        wide_f32(TILES, ROWS),
        pltpu.VMEM((ROWS, COLS), bf16),
        wide_f32(16, ROWS),
        wide_f32(ROWS),
        wide_f32(ROWS),
        wide_f32(2, PIECE),
        wide_f32(TILES),
        wide_f32(LINES),
        wide_f32(TILES),
        wide_f32(ITERS, 8, LINES),
        wide_f32(ITERS, 16, TILES),
        wide_f32(8, LINES + 8),
        wide_f32(16, 8),
        wide_f32(2, LINES),
        wide_f32(2, LINES),
        wide_f32(4, half),
        wide_bf16(4, half), wide_bf16(2, 4, half), wide_bf16(4, 2, part), wide_bf16(2, 4, half),
        wide_bf16(3, half), wide_bf16(2, half), wide_bf16(2, part), wide_bf16(half),
        wide_bf16(4, half), wide_bf16(4, 2, part), wide_bf16(2, 4, half), wide_bf16(2, 4, half),
        wide_bf16(4, half),
        wide_bf16(2, half), wide_bf16(2, 2, part), wide_bf16(2, 2, half), wide_bf16(2, 2, half),
        dma((WIRES,)),
        dma((WIRES,)),
    ]
    return pl.pallas_call(
        kernel,
        out_shape=(
            jax.ShapeDtypeStruct((OWNED, LANES), f32),
            jax.ShapeDtypeStruct((2, LINES, LANES), f32),
            jax.ShapeDtypeStruct((LINES, LANES), f32),
            jax.ShapeDtypeStruct((1, 1), f32),
        ),
        in_specs=[pl.BlockSpec(memory_space=pltpu.SMEM), vmem, vmem],
        out_specs=(vmem,) * 4,
        scratch_shapes=scratch,
        compiler_params=pltpu.CompilerParams(
            collective_id=0, has_side_effects=True, vmem_limit_bytes=62 * 2**20
        ),
    )(band_start, student, teacher)


def local(student, teacher, band_start):
    grad, stu, tea, loss = one_device(band_start, student, teacher)
    return (grad, stu.reshape(OWNED), tea.reshape(PIECE), loss.reshape(()))


def solution(mesh):
    placed = (P("stu", "tea"), P("tea", "stu"), P())
    return jax.shard_map(
        local,
        mesh=mesh,
        in_specs=placed,
        out_specs=(P("stu", "tea"), P("stu"), P("tea"), P()),
        check_vma=False,
    )
```

```python
import functools
import math

import jax
import jax.numpy as jnp
from jax import lax
from jax.experimental import pallas as pl
from jax.experimental.pallas import tpu as pltpu
from jax.sharding import PartitionSpec as P

D = 2048
BLK = 512
W = 4
ITERS = 3
LANES = 128
OWNED = 2048
ROWS = 1024
COLS = 2048
PIECE = 1024
TILES = COLS // LANES
LINES = ROWS // LANES
TOKENS = 16384
GA, GB = 768, 256
QA, QB = 640, 384
WIRES = 300
UP, DOWN = 1, 3

epsilon = 0.02
kappa = math.log2(math.e) / epsilon
log2e = math.log2(math.e)
log2_tokens = math.log2(TOKENS)
unlisted = -1e30
MESH = pl.DeviceIdType.MESH
f32 = jnp.float32
bf16 = jnp.bfloat16


def aligned(start, size):
    return pl.ds(pl.multiple_of(start, size), size)


def total_of(parts):
    return functools.reduce(lambda a, b: a + b, parts)


def merge(parts):
    highest = functools.reduce(jnp.maximum, parts)
    return highest + jnp.log(total_of([jnp.exp2(p - highest) for p in parts])) * log2e


class Place:
    def __init__(self):
        self.s = lax.axis_index("stu")
        self.t = lax.axis_index("tea")
        self.y = lax.div(self.s, 2)
        self.core = lax.rem(self.s, 2)
        self.z = lax.div(self.t, 4)
        self.x = lax.rem(self.t, 4)
        self.h = lax.rem(self.x, 2)
        self.l = lax.div(self.x, 2)
        self.row_slot = 2 * self.z + self.l
        self.col_slot = 2 * self.s + self.h

    def zi(self, dz):
        return lax.rem(self.z + dz, 4)

    def yi(self, dy):
        return lax.rem(self.y + dy, 4)

    def xi(self, dx):
        return lax.rem(self.x + dx, 4)

    def tea(self, dz, dx):
        return self.zi(dz) * 4 + self.xi(dx)

    def stu(self, dy):
        return lax.rem(self.y + dy, 4) * 2 + self.core

    def at_x(self, d):
        return (self.s, self.tea(0, d))

    def at_z(self, d):
        return (self.s, self.tea(d, 0))

    def at_y(self, d):
        return (self.stu(d), self.t)

    def sibling(self):
        return (self.y * 2 + 1 - self.core, self.t)

    def partner(self):
        return (self.s, self.z * 4 + self.l * 2 + 1 - self.h)

    def outer(self):
        return (self.s, self.z * 4 + lax.rem(self.x + 3 + 2 * self.h, 4))

    def at_row(self, d):
        k = lax.rem(self.row_slot + d, 8)
        return (self.s, lax.div(k, 2) * 4 + lax.rem(k, 2) * 2 + self.h)

    def at_col(self, d):
        k = lax.rem(self.col_slot + d, 16)
        return (lax.div(k, 2), self.z * 4 + self.l * 2 + lax.rem(k, 2))


class Wire:
    def __init__(self, send, recv):
        self.send, self.recv, self.used, self.open = send, recv, 0, []

    def start(self, src, dst, device):
        copy = pltpu.make_async_remote_copy(
            src_ref=src, dst_ref=dst,
            send_sem=self.send.at[self.used], recv_sem=self.recv.at[self.used],
            device_id=device, device_id_type=MESH,
        )
        self.used += 1
        copy.start()
        self.open.append(copy)
        return copy

    def drain(self):
        for copy in self.open:
            copy.wait_send()
        self.open = []


WAYS = ((UP, DOWN, 0), (DOWN, UP, 1))


def gather(me, wire, stu_other, own_here, S, T, X, relay_a, relay_b, part_sq, ysq_row, cost):
    A, B = pl.ds(0, GA), pl.ds(GA, GB)
    a_part = [pl.ds(0, GA // 2), pl.ds(GA // 2, GA // 2)]
    b_part = [pl.ds(GA, GB // 2), pl.ds(GA + GB // 2, GB // 2)]
    x_part = [pl.ds(0, GB // 2), pl.ds(GB // 2, GB // 2)]
    t_part = [pl.ds(0, PIECE // 2), pl.ds(PIECE // 2, PIECE // 2)]

    def push(ref, device):
        return wire.start(ref, ref, device)

    def piece(dz, dx, rows):
        return S.at[me.tea(dz, dx), rows]

    def t_push(dy, e, rows, device):
        return push(T.at[me.stu(dy), e, rows], device)

    own, other = me.h, 1 - me.h
    ty, tyf = {}, {0: [], 1: []}
    tc = {(order, d): [] for order in range(2) for d in (0, UP, DOWN, 2)}

    def t_spread(order, e, parts):
        for keep in parts:
            way = WAYS[keep][0]
            ty[order, way, 0] = t_push(0, e, t_part[keep], me.at_y(way))
        for keep in parts:
            way = WAYS[1 - keep][0]
            ty[order, way, 1] = t_push(0, e, t_part[keep], me.at_y(way))
            tc[order, 0].append(t_push(0, e, t_part[keep], me.sibling()))

    own_here()
    ax, ar, axf, az, azf = {}, {}, {}, {}, []
    bz, bzf, bx, br, bxf = {}, [], {}, {}, {}
    for way, back, keep in WAYS:
        ar[way] = wire.start(S.at[me.t, a_part[keep]], relay_a.at[keep], me.at_x(way))
    t_spread(0, own, (0, 1))
    for way, back, keep in WAYS:
        ax[way] = wire.start(stu_other.at[A], S.at[me.t, A], me.at_x(way))
    tp = [t_push(0, own, t_part[keep], me.partner()) for keep in range(2)]

    def turn_a(dx):
        for way, back, keep in WAYS:
            az[dx, way, 0] = push(piece(0, dx, a_part[keep]), me.at_z(way))
        for way, back, keep in WAYS:
            az[dx, way, 1] = push(piece(0, dx, a_part[1 - keep]), me.at_z(way))

    def turn_b(dz):
        for way, back, keep in WAYS:
            br[dz, way] = wire.start(
                piece(dz, 0, b_part[keep]), relay_b.at[me.zi(dz), keep], me.at_x(way)
            )
        for way in (UP, DOWN):
            bx[dz, way] = wire.start(X.at[me.zi(dz)], piece(dz, 0, B), me.at_x(way))

    turn_a(0)
    own_squares(me, T, part_sq)
    squares = tell(wire, part_sq, me.col_slot, 16, me.at_col)
    for way in (UP, DOWN):
        bz[way] = (push(piece(0, 0, B), me.at_z(way)), push(X.at[me.z], me.at_z(way)))

    for way, back, keep in WAYS:
        ar[way].wait_recv()
        axf[way] = wire.start(relay_a.at[keep], piece(0, back, a_part[keep]), me.at_x(way))
    for way, back, keep in WAYS:
        ax[way].wait_recv()
        turn_a(back)

    def t_relay(order, e):
        for way, back, keep in WAYS:
            ty[order, way, 0].wait_recv()
            tyf[order].append(t_push(back, e, t_part[keep], me.at_y(way)))
        for way, back, keep in WAYS:
            ty[order, way, 1].wait_recv()
            tc[order, back].append(t_push(back, e, pl.ds(0, PIECE), me.sibling()))

    def t_last(order, e):
        for keep, copy in enumerate(tyf[order]):
            copy.wait_recv()
            tc[order, 2].append(t_push(2, e, t_part[keep], me.sibling()))

    for copy in axf.values():
        copy.wait_recv()
    turn_a(2)
    for way, back, keep in WAYS:
        for copy in bz[way]:
            copy.wait_recv()
        bzf.append(push(piece(back, 0, b_part[keep]), me.at_z(way)))
        bzf.append(push(X.at[me.zi(back), x_part[keep]], me.at_z(way)))
    t_relay(0, own)
    for copy in tp:
        copy.wait_recv()
    t_spread(1, other, (0, 1))
    turn_b(0)
    turn_b(DOWN)
    turn_b(UP)
    for copy in bzf:
        copy.wait_recv()
    turn_b(2)

    def b_relay(dz):
        bxf[dz] = []
        for way, back, keep in WAYS:
            br[dz, way].wait_recv()
            bxf[dz].append(
                wire.start(relay_b.at[me.zi(dz), keep], piece(dz, back, b_part[keep]), me.at_x(way))
            )

    def a_relay(dx):
        for way, back, keep in WAYS:
            az[dx, way, 0].wait_recv()
            azf.append(push(piece(back, dx, a_part[keep]), me.at_z(way)))

    def b_here(dz):
        for way in (UP, DOWN):
            bx[dz, way].wait_recv()
        for copy in bxf[dz]:
            copy.wait_recv()

    def t_here(order, *places):
        for d in places:
            for copy in tc[order, d]:
                copy.wait_recv()

    def a_here(*places):
        for dx in places:
            for way in (UP, DOWN):
                az[dx, way, 1].wait_recv()

    a_relay(0)
    t_last(0, own)
    a_relay(DOWN)
    a_relay(UP)
    b_relay(0)
    b_relay(DOWN)
    b_relay(UP)
    t_here(0, 0, UP, DOWN, 2)
    b_here(0)
    cost([me.zi(0)], own, first=True)
    a_relay(2)
    b_relay(2)
    t_relay(1, other)
    a_here(0, UP, DOWN, 2)
    b_here(DOWN)
    b_here(UP)
    cost([me.zi(DOWN), me.zi(UP)], own)
    for copy in azf + squares:
        copy.wait_recv()
    for e in range(2):
        ysq_row[e * PIECE // LANES:(e + 1) * PIECE // LANES, :] = total_of(
            [part_sq[2 * i + e] for i in range(8)]
        )
    b_here(2)
    cost([me.zi(2)], own, last=True, new_rows=True)
    t_last(1, other)
    t_here(1, 0, UP, DOWN)
    cost([me.yi(0), me.yi(DOWN), me.yi(UP)], other, first=True)
    t_here(1, 2)
    cost([me.yi(2)], other, last=True)


def own_squares(me, T, part_sq):
    def block(b, carry):
        rows = aligned(b * LANES, LANES)
        squared = total_of([
            jnp.square(T[me.s, me.h, rows, side * LANES:(side + 1) * LANES].astype(f32))
            for side in range(2)
        ])
        part_sq[me.col_slot, pl.ds(b, 1), :] = jnp.sum(squared.T, axis=0, keepdims=True)
        return carry

    lax.fori_loop(0, PIECE // LANES, block, 0)


def cost_of(me, band, S, T, z, xsq, ysq_row):
    scale = kappa / D

    def cost(groups, e, first=False, last=False, new_rows=False):
        def cols_block(n, carry):
            cols = aligned(n * 256, 256)
            rhs = jnp.concatenate(
                [T[2 * group + i, e, cols, :] for group in groups for i in range(2)], axis=1
            )
            lhs = jnp.concatenate(
                [S[4 * group + i] for group in groups for i in range(4)], axis=1
            )
            prod = lax.dot_general(
                lhs, rhs, (((1,), (1,)), ((), ())), preferred_element_type=f32
            )
            for side in range(2):
                at = e * (TILES // 2) + 2 * n + side
                block = me.row_slot * 4 + e * 2 + lax.div(n, 2)
                for half in range(2):
                    rows = pl.ds(half * BLK, BLK)
                    tile = prod[half * BLK:(half + 1) * BLK, side * LANES:(side + 1) * LANES]
                    tile = tile if first else z[at, rows, :] + tile
                    if last:
                        lowest = band[me.s * 4 + me.h * 2 + half]
                        lowest = jnp.full((BLK, LANES), lowest, jnp.int32)
                        here = jnp.full((BLK, LANES), block, jnp.int32)
                        listed = (here >= lowest) & (here < lowest + W)
                        tile = (2.0 * tile - xsq[rows, :] - ysq_row[pl.ds(at, 1), :]) * scale
                        tile = jnp.where(listed, tile, unlisted)
                    z[at, rows, :] = tile
            return carry

        def squares_block(b, carry):
            rows = aligned(b * LANES, LANES)
            squared = total_of([jnp.square(S[i, rows, :].astype(f32)) for i in range(16)])
            xsq[rows, :] = jnp.broadcast_to(
                jnp.sum(squared, axis=1, keepdims=True), (LANES, LANES)
            )
            return carry

        if new_rows:
            lax.fori_loop(0, LINES, squares_block, 0)
        lax.fori_loop(0, PIECE // 256, cols_block, 0)

    return cost


def spread_lines(compact, tall):
    for c in range(TILES):
        tall[c] = jnp.broadcast_to(compact[c:c + 1, :], (8, LANES))


def row_stats(z, tall, lane_high, lane_total, put):
    def lanes(b, carry):
        for part in range(4):
            rows = aligned(b * 64 + part * 16, 16)
            scores = [z[c, rows, :].reshape(2, 8, LANES) + tall[c][None] for c in range(TILES)]
            high = functools.reduce(jnp.maximum, scores)
            lane_high[rows, :] = high.reshape(16, LANES)
            lane_total[rows, :] = total_of([jnp.exp2(v - high) for v in scores]).reshape(16, LANES)
        return carry

    lax.fori_loop(0, ROWS // 64, lanes, 0)

    def block(b, carry):
        rows = aligned(b * LANES, LANES)
        value = (lane_high[rows, :] + jnp.log(lane_total[rows, :]) * log2e).T
        top = jnp.max(value, axis=0, keepdims=True)
        total = jnp.sum(jnp.exp2(value - top), axis=0, keepdims=True)
        put(b, top + jnp.log(total) * log2e)
        return carry

    lax.fori_loop(0, LINES, block, 0, unroll=True)


def spread_rows(compact, wide):
    def block(b, carry):
        line = jnp.broadcast_to(compact[pl.ds(b, 1), :], (LANES, LANES))
        wide[aligned(b * LANES, LANES), :] = line.T
        return carry

    lax.fori_loop(0, LINES, block, 0, unroll=True)


def col_stats(z, wide, put):
    def tiles(cc, carry):
        highs = [jnp.full((8, LANES), unlisted, f32) for _ in range(4)]
        totals = [jnp.zeros((8, LANES), f32) for _ in range(4)]
        for b in range(ROWS // 64):
            rows = pl.ds(b * 64, 64)
            pot = wide[rows, :]
            for k in range(4):
                scores = (z[cc * 4 + k, rows, :] + pot).reshape(8, 8, LANES)
                new = jnp.maximum(highs[k], jnp.max(scores, axis=0))
                totals[k] = totals[k] * jnp.exp2(highs[k] - new) + jnp.sum(
                    jnp.exp2(scores - new[None]), axis=0
                )
                highs[k] = new
        for k in range(4):
            top = jnp.max(highs[k], axis=0, keepdims=True)
            total = jnp.sum(totals[k] * jnp.exp2(highs[k] - top), axis=0, keepdims=True)
            put(cc * 4 + k, top + jnp.log(total) * log2e)
        return carry

    lax.fori_loop(0, TILES // 4, tiles, 0)


def tell(wire, slots, index, count, peer):
    return [wire.start(slots.at[index], slots.at[index], peer(d)) for d in range(1, count)]


def swap(wire, slots, index, count, peer):
    for copy in tell(wire, slots, index, count, peer):
        copy.wait_recv()


def sweeps(me, wire, z, wide, stu, tea, tall, row_l, col_l, lane_high, lane_total):
    tea[...] = jnp.zeros_like(tea)
    for sweep in range(ITERS):
        rl, cl = row_l.at[sweep], col_l.at[sweep]

        def put_row(b, value):
            rl[me.row_slot, pl.ds(b, 1), :] = value

        spread_lines(tea, tall)
        row_stats(z, tall, lane_high, lane_total, put_row)
        swap(wire, rl, me.row_slot, 8, me.at_row)
        stu[...] = -log2_tokens - merge([rl[i] for i in range(8)])
        spread_rows(stu, wide)

        def put_col(c, value):
            cl[me.col_slot, pl.ds(c, 1), :] = value

        col_stats(z, wide, put_col)
        swap(wire, cl, me.col_slot, 16, me.at_col)
        tea[...] = -log2_tokens - merge([cl[i] for i in range(16)])


def make_plan(me, z, wide, tall, xsq, ysq_tall, w, sum_r, lane_mass, lane_pull):
    def lanes(b, loss):
        for part in range(4):
            rows = aligned(b * 64 + part * 16, 16)
            pot = (wide[rows, :] + log2_tokens).reshape(2, 8, LANES)
            mass, pull = [], []
            for c in range(TILES):
                tile = z[c, rows, :].reshape(2, 8, LANES)
                scaled = jnp.exp2(tile + pot + tall[c][None])
                loss = loss + total_of([scaled[i] * tile[i] for i in range(2)])
                rounded = scaled.reshape(16, LANES).astype(bf16)
                w[rows, c * LANES:(c + 1) * LANES] = rounded
                rounded = rounded.astype(f32).reshape(2, 8, LANES)
                mass.append(rounded)
                pull.append(rounded * (ysq_tall[c][None] + (D / kappa) * tile))
            lane_mass[rows, :] = total_of(mass).reshape(16, LANES)
            lane_pull[rows, :] = total_of(pull).reshape(16, LANES)
        return loss

    loss = lax.fori_loop(0, ROWS // 64, lanes, jnp.zeros((8, LANES), f32))

    def block(b, carry):
        rows = aligned(b * LANES, LANES)
        mass = jnp.sum(lane_mass[rows, :].T, axis=0, keepdims=True)
        pull = jnp.sum(lane_pull[rows, :].T, axis=0, keepdims=True)
        own = xsq[rows, :].T[0:1, :]
        usable = own > 1e-20
        gamma = jnp.where(usable, 0.5 * (mass + pull / jnp.where(usable, own, 1.0)), 0.0)
        wide[rows, :] = jnp.broadcast_to(gamma, (LANES, LANES)).T
        sum_r[me.row_slot, pl.ds(b, 1), :] = mass - gamma
        return carry

    lax.fori_loop(0, LINES, block, 0, unroll=True)
    sum_r[me.row_slot, LINES:LINES + 8, :] = loss


def pull_of(S, T, w, wide, G):
    def pull(q, part):
        def rows_block(rows):
            prod = jnp.dot(
                w[rows, :], T[q].reshape(COLS, 2 * LANES), preferred_element_type=f32
            )
            gamma = wide[rows, :]
            for side in range(2):
                own = S[2 * q + side, rows, :].astype(f32)
                G[2 * q + side, rows, :] = gamma * own - prod[:, side * LANES:(side + 1) * LANES]

        if part == 0:
            def block(r, carry):
                rows_block(aligned(r * (QA // 2), QA // 2))
                return carry

            lax.fori_loop(0, 2, block, 0)
        else:
            rows_block(pl.ds(QA, QB))

    return pull


def add(dst, terms):
    def block(r, carry):
        rows = aligned(r * 64, 64)
        dst[rows, :] = total_of([term[rows, :].astype(f32) for term in terms]).astype(dst.dtype)
        return carry

    lax.fori_loop(0, dst.shape[0] // 64, block, 0)


def in_two(rows):
    return (pl.ds(0, rows // 2), pl.ds(rows // 2, rows // 2))


def reduce_a(me, wire, G, pull, far_out, near_out, far_in, near_in, x_out, x_in, x_relay, x_far):
    PARTS = in_two(QA)

    def value(t):
        return G.at[t, pl.ds(0, QA)]

    def pull_to(dz):
        for k in range(2):
            pull(2 * me.zi(dz) + k, 0)

    pull_to(2)
    far = []
    for j in range(4):
        add(far_out.at[j], [value(me.zi(2) * 4 + j)])
        far.append([
            wire.start(far_out.at[j, PARTS[keep]], far_in.at[j, keep], me.at_z(way))
            for way, back, keep in WAYS
        ])
    yield
    pull_to(UP)
    pull_to(DOWN)
    near = []
    for j in range(4):
        for way, back, keep in WAYS:
            far[j][keep].wait_recv()
            chained, direct = PARTS[keep], PARTS[1 - keep]
            mine = value(me.zi(way) * 4 + j)
            out = near_out.at[keep, j]
            add(out.at[chained], [mine.at[chained], far_in.at[j, keep]])
            add(out.at[direct], [mine.at[direct]])
            near.append(wire.start(out, near_in.at[keep, j], me.at_z(way)))
    yield
    pull_to(0)
    for copy in near:
        copy.wait_recv()
    for j in range(4):
        mine = value(me.z * 4 + j)
        add(mine, [mine, near_in.at[0, j], near_in.at[1, j]])
    add(x_out.at[2], [value(me.tea(0, 2))])
    far = [
        wire.start(x_out.at[2, PARTS[keep]], x_relay.at[keep], me.at_x(way))
        for way, back, keep in WAYS
    ]
    near = []
    for way, back, keep in WAYS:
        add(x_out.at[keep], [value(me.tea(0, way))])
        near.append(wire.start(x_out.at[keep], x_in.at[keep], me.at_x(way)))
    yield
    last = []
    for way, back, keep in WAYS:
        far[keep].wait_recv()
        last.append(wire.start(x_relay.at[keep], x_far.at[PARTS[keep]], me.at_x(way)))
    yield
    for copy in near + last:
        copy.wait_recv()
    yield


def reduce_b(
    me, wire, G, pull, far_out, relay, x_out, x_in, x_far, others,
    z_far_out, z_far_in, z_out, z_in,
):
    PARTS = in_two(QB)
    order = (2, UP, DOWN, 0)

    def value(t):
        return G.at[t, pl.ds(QA, QB)]

    far, near, last = {}, {}, {}
    for dz in order:
        pull(2 * me.zi(dz) + 1 - me.l, 1)
        add(far_out.at[me.zi(dz)], [value(me.tea(dz, 2))])
        far[dz] = [
            wire.start(
                far_out.at[me.zi(dz), PARTS[keep]], relay.at[me.zi(dz), keep], me.at_x(way)
            )
            for way, back, keep in WAYS
        ]
    yield
    for dz in order:
        pull(2 * me.zi(dz) + me.l, 1)
        near[dz] = []
        for way, back, keep in WAYS:
            add(x_out.at[keep, me.zi(dz)], [value(me.tea(dz, way))])
            near[dz].append(
                wire.start(x_out.at[keep, me.zi(dz)], x_in.at[keep, me.zi(dz)], me.at_x(way))
            )
        last[dz] = []
        for way, back, keep in WAYS:
            far[dz][keep].wait_recv()
            last[dz].append(
                wire.start(relay.at[me.zi(dz), keep], x_far.at[me.zi(dz), PARTS[keep]], me.at_x(way))
            )
    yield

    def arrived(dz):
        for copy in near[dz] + last[dz]:
            copy.wait_recv()
        mine, other = value(me.tea(dz, 0)), others.at[me.zi(dz)]
        add(mine, [mine, x_far.at[me.zi(dz)]])
        add(other, [x_in.at[0, me.zi(dz)], x_in.at[1, me.zi(dz)]])
        return mine, other

    z_far = {}
    for i, term in enumerate(arrived(2)):
        add(z_far_out.at[i], [term])
        for way, back, keep in WAYS:
            z_far[i, way] = wire.start(
                z_far_out.at[i, PARTS[keep]], z_far_in.at[i, keep], me.at_z(way)
            )
    yield
    z_near = []
    terms = {way: arrived(way) for way in (UP, DOWN)}
    for i in range(2):
        for way, back, keep in WAYS:
            z_far[i, way].wait_recv()
            chained, direct = PARTS[keep], PARTS[1 - keep]
            term, out = terms[way][i], z_out.at[i, keep]
            add(out.at[chained], [term.at[chained], z_far_in.at[i, keep]])
            add(out.at[direct], [term.at[direct]])
            z_near.append(wire.start(out, z_in.at[i, keep], me.at_z(way)))
    yield
    terms = arrived(0)
    for copy in z_near:
        copy.wait_recv()
    for i, term in enumerate(terms):
        add(term, [term, z_in.at[i, 0], z_in.at[i, 1]])
    yield


def kernel(
    band, stu_in, tea_in, grad_out, stu_out, tea_out, loss,
    S, T, X, stu_other, grad, relay_a, relay_b, z, w, G, wide, xsq, xsq_other, part_sq, ysq_row, stu, tea, tall, ysq_tall,
    row_l, col_l, sum_r, sum_c, pair_f, pair_b, others,
    a_far_out, a_near_out, a_far_in, a_near_in, a_x_out, a_x_in, a_x_relay, a_x_far,
    b_far_out, b_relay, b_x_out, b_x_in, b_x_far, b_z_far_out, b_z_far_in, b_z_out, b_z_in,
    send, recv, here,
):
    me = Place()
    mine = pl.multiple_of(me.h * ROWS, ROWS)
    other = pl.multiple_of((1 - me.h) * ROWS, ROWS)
    loads = [
        pltpu.make_async_copy(tea_in, T.at[me.s, me.h], here.at[0]),
        pltpu.make_async_copy(stu_in.at[pl.ds(mine, ROWS)], S.at[me.t], here.at[1]),
        pltpu.make_async_copy(stu_in.at[pl.ds(other, ROWS)], stu_other, here.at[2]),
        pltpu.make_async_copy(stu_in.at[pl.ds(other + GA, GB)], X.at[me.z], here.at[3]),
    ]
    for copy in loads:
        copy.start()
    barrier = pltpu.get_barrier_semaphore()
    peers = [me.outer()] + [me.at_row(d) for d in range(1, 8)] + [me.at_col(d) for d in range(1, 16)]
    for peer in peers:
        pl.semaphore_signal(barrier, inc=1, device_id=peer, device_id_type=MESH)

    def own_here():
        for copy in loads:
            copy.wait()
        pl.semaphore_wait(barrier, len(peers))

    wire = Wire(send, recv)
    gather(
        me, wire, stu_other, own_here, S, T, X, relay_a, relay_b, part_sq, ysq_row,
        cost_of(me, band, S, T, z, xsq, ysq_row),
    )
    sweeps(me, wire, z, wide, stu, tea, tall, row_l, col_l, G.at[0], G.at[1])
    spread_lines(tea, tall)
    spread_lines(ysq_row, ysq_tall)
    make_plan(me, z, wide, tall, xsq, ysq_tall, w, sum_r, G.at[0], G.at[1])
    sums = tell(wire, sum_r, me.row_slot, 8, me.at_row)
    pair_f[me.h] = stu[...] / kappa
    sums.append(wire.start(pair_f.at[me.h], pair_f.at[me.h], me.partner()))
    tea[...] = tea[...] / kappa
    stores = [
        pltpu.make_async_copy(tea.at[aligned(me.h * LINES, LINES)], tea_out, here.at[4])
    ]
    stores[-1].start()
    pull = pull_of(S, T, w, wide, G)
    first = reduce_a(
        me, wire, G, pull, a_far_out, a_near_out, a_far_in, a_near_in,
        a_x_out, a_x_in, a_x_relay, a_x_far,
    )
    second = reduce_b(
        me, wire, G, pull, b_far_out, b_relay, b_x_out, b_x_in, b_x_far, others,
        b_z_far_out, b_z_far_in, b_z_out, b_z_in,
    )
    steps = [first, second] * 3 + [second, first, second, first]
    for number, step in enumerate(steps):
        next(step)
        if number == 1:
            for copy in sums:
                copy.wait_recv()
            summed = total_of([sum_r[i] for i in range(8)])
            sum_c[me.col_slot] = summed[LINES:, :]
            pair_b[me.h] = summed[:LINES, :]
            sums = tell(wire, sum_c, me.col_slot, 16, me.at_col)
            sums.append(wire.start(pair_b.at[me.h], pair_b.at[me.h], me.partner()))
            stores.append(pltpu.make_async_copy(pair_f, stu_out, here.at[5]))
            stores[-1].start()
        if number == 3:
            for copy in sums:
                copy.wait_recv()
            total = total_of([sum_c[i] for i in range(16)])
            total = jnp.sum(jnp.sum(total, axis=0, keepdims=True), axis=1, keepdims=True)
            loss[...] = total * (-1.0 / (kappa * TOKENS))
            spread_rows(pair_b.at[me.h], xsq)
            spread_rows(pair_b.at[1 - me.h], xsq_other)

    def finish(first_row, rows_total, own_terms, other_terms, at):
        def block(r, carry):
            near = aligned(r * LANES, LANES)
            rows = aligned(first_row + r * LANES, LANES)
            grad[aligned(mine + first_row + r * LANES, LANES), :] = (
                xsq[rows, :] * S[me.t, rows, :].astype(f32)
                + total_of([term[near, :].astype(f32) for term in own_terms])
            )
            grad[aligned(other + first_row + r * LANES, LANES), :] = (
                xsq_other[rows, :] * stu_other[rows, :].astype(f32)
                + total_of([term[near, :].astype(f32) for term in other_terms])
            )
            return carry

        lax.fori_loop(0, rows_total // LANES, block, 0)
        for i, base in enumerate((mine, other)):
            rows = aligned(base + first_row, LANES)
            rows = pl.ds(rows.start, rows_total)
            stores.append(
                pltpu.make_async_copy(grad.at[rows], grad_out.at[rows], here.at[at + i])
            )
            stores[-1].start()

    finish(0, QA, [G.at[me.t, pl.ds(0, QA)], a_x_far], [a_x_in.at[0], a_x_in.at[1]], 6)
    finish(QA, QB, [G.at[me.t, pl.ds(QA, QB)]], [others.at[me.z]], 8)
    wire.drain()
    for copy in stores:
        copy.wait()


def one_device(band_start, student, teacher):
    dma = pltpu.SemaphoreType.DMA
    vmem = pl.BlockSpec(memory_space=pltpu.VMEM)
    anywhere = pl.BlockSpec(memory_space=pl.ANY)

    def wide_bf16(*lead):
        return pltpu.VMEM((*lead, LANES), bf16)

    def wide_f32(*lead):
        return pltpu.VMEM((*lead, LANES), f32)

    scratch = [
        wide_bf16(16, ROWS),
        pltpu.VMEM((8, 2, PIECE, 2 * LANES), bf16),
        wide_bf16(4, GB),
        wide_bf16(ROWS),
        wide_f32(OWNED),
        wide_bf16(2, GA // 2),
        wide_bf16(4, 2, GB // 2),
        wide_f32(TILES, ROWS),
        pltpu.VMEM((ROWS, COLS), bf16),
        wide_f32(16, ROWS),
        wide_f32(ROWS),
        wide_f32(ROWS),
        wide_f32(ROWS),
        wide_f32(16, PIECE // LANES),
        wide_f32(TILES),
        wide_f32(LINES),
        wide_f32(TILES),
        wide_f32(TILES, 8),
        wide_f32(TILES, 8),
        wide_f32(ITERS, 8, LINES),
        wide_f32(ITERS, 16, TILES),
        wide_f32(8, LINES + 8),
        wide_f32(16, 8),
        wide_f32(2, LINES),
        wide_f32(2, LINES),
        wide_f32(4, QB),
        wide_bf16(4, QA), wide_bf16(2, 4, QA), wide_bf16(4, 2, QA // 2), wide_bf16(2, 4, QA),
        wide_bf16(3, QA), wide_bf16(2, QA), wide_bf16(2, QA // 2), wide_bf16(QA),
        wide_bf16(4, QB), wide_bf16(4, 2, QB // 2), wide_bf16(2, 4, QB), wide_bf16(2, 4, QB),
        wide_bf16(4, QB),
        wide_bf16(2, QB), wide_bf16(2, 2, QB // 2), wide_bf16(2, 2, QB), wide_bf16(2, 2, QB),
        dma((WIRES,)),
        dma((WIRES,)),
        dma((10,)),
    ]
    return pl.pallas_call(
        kernel,
        out_shape=(
            jax.ShapeDtypeStruct((OWNED, LANES), f32),
            jax.ShapeDtypeStruct((2, LINES, LANES), f32),
            jax.ShapeDtypeStruct((LINES, LANES), f32),
            jax.ShapeDtypeStruct((1, 1), f32),
        ),
        in_specs=[pl.BlockSpec(memory_space=pltpu.SMEM), anywhere, anywhere],
        out_specs=(anywhere, anywhere, anywhere, vmem),
        scratch_shapes=scratch,
        compiler_params=pltpu.CompilerParams(
            collective_id=0, has_side_effects=True, vmem_limit_bytes=62 * 2**20
        ),
    )(band_start, student, teacher)


def local(student, teacher, band_start):
    grad, stu, tea, loss = one_device(band_start, student, teacher)
    return (grad, stu.reshape(OWNED), tea.reshape(PIECE), loss.reshape(()))


def solution(mesh):
    placed = (P("stu", "tea"), P("tea", "stu"), P())
    return jax.shard_map(
        local,
        mesh=mesh,
        in_specs=placed,
        out_specs=(P("stu", "tea"), P("stu"), P("tea"), P()),
        check_vma=False,
    )
```

```python
import functools
import math

import jax
import jax.numpy as jnp
from jax import lax
from jax.experimental import pallas as pl
from jax.experimental.pallas import tpu as pltpu
from jax.sharding import PartitionSpec as P

D = 2048
BLK = 512
W = 4
ITERS = 3
LANES = 128
OWNED = 2048
ROWS = 1024
COLS = 2048
PIECE = 1024
TILES = COLS // LANES
LINES = ROWS // LANES
TOKENS = 16384
GA, GB = 768, 256
QA, QB = 640, 384
WIRES = 300
UP, DOWN = 1, 3

epsilon = 0.02
kappa = math.log2(math.e) / epsilon
log2e = math.log2(math.e)
log2_tokens = math.log2(TOKENS)
unlisted = -1e30
MESH = pl.DeviceIdType.MESH
f32 = jnp.float32
bf16 = jnp.bfloat16


def aligned(start, size):
    return pl.ds(pl.multiple_of(start, size), size)


def total_of(parts):
    return functools.reduce(lambda a, b: a + b, parts)


def merge(parts):
    highest = functools.reduce(jnp.maximum, parts)
    return highest + jnp.log(total_of([jnp.exp2(p - highest) for p in parts])) * log2e


class Place:
    def __init__(self):
        self.s = lax.axis_index("stu")
        self.t = lax.axis_index("tea")
        self.y = lax.div(self.s, 2)
        self.core = lax.rem(self.s, 2)
        self.z = lax.div(self.t, 4)
        self.x = lax.rem(self.t, 4)
        self.h = lax.rem(self.x, 2)
        self.l = lax.div(self.x, 2)
        self.row_slot = 2 * self.z + self.l
        self.col_slot = 2 * self.s + self.h

    def zi(self, dz):
        return lax.rem(self.z + dz, 4)

    def yi(self, dy):
        return lax.rem(self.y + dy, 4)

    def xi(self, dx):
        return lax.rem(self.x + dx, 4)

    def tea(self, dz, dx):
        return self.zi(dz) * 4 + self.xi(dx)

    def stu(self, dy):
        return lax.rem(self.y + dy, 4) * 2 + self.core

    def at_x(self, d):
        return (self.s, self.tea(0, d))

    def at_z(self, d):
        return (self.s, self.tea(d, 0))

    def at_y(self, d):
        return (self.stu(d), self.t)

    def sibling(self):
        return (self.y * 2 + 1 - self.core, self.t)

    def partner(self):
        return (self.s, self.z * 4 + self.l * 2 + 1 - self.h)

    def outer(self):
        return (self.s, self.z * 4 + lax.rem(self.x + 3 + 2 * self.h, 4))

    def at_row(self, d):
        k = lax.rem(self.row_slot + d, 8)
        return (self.s, lax.div(k, 2) * 4 + lax.rem(k, 2) * 2 + self.h)

    def at_col(self, d):
        k = lax.rem(self.col_slot + d, 16)
        return (lax.div(k, 2), self.z * 4 + self.l * 2 + lax.rem(k, 2))


class Wire:
    def __init__(self, send, recv):
        self.send, self.recv, self.used, self.open = send, recv, 0, []

    def start(self, src, dst, device):
        copy = pltpu.make_async_remote_copy(
            src_ref=src, dst_ref=dst,
            send_sem=self.send.at[self.used], recv_sem=self.recv.at[self.used],
            device_id=device, device_id_type=MESH,
        )
        self.used += 1
        copy.start()
        self.open.append(copy)
        return copy

    def drain(self):
        for copy in self.open:
            copy.wait_send()
        self.open = []


WAYS = ((UP, DOWN, 0), (DOWN, UP, 1))


def gather(me, wire, stu_other, own_here, S, T, X, relay_a, relay_b, part_sq, ysq_row, cost):
    A, B = pl.ds(0, GA), pl.ds(GA, GB)
    a_part = [pl.ds(0, GA // 2), pl.ds(GA // 2, GA // 2)]
    b_part = [pl.ds(GA, GB // 2), pl.ds(GA + GB // 2, GB // 2)]
    x_part = [pl.ds(0, GB // 2), pl.ds(GB // 2, GB // 2)]
    t_part = [pl.ds(0, PIECE // 2), pl.ds(PIECE // 2, PIECE // 2)]

    def push(ref, device):
        return wire.start(ref, ref, device)

    def piece(dz, dx, rows):
        return S.at[me.tea(dz, dx), rows]

    def t_push(dy, e, rows, device):
        return push(T.at[me.stu(dy), e, rows], device)

    own, other = me.h, 1 - me.h
    ty, tyf = {}, {0: [], 1: []}
    tc = {(order, d): [] for order in range(2) for d in (0, UP, DOWN, 2)}

    def t_spread(order, e, parts):
        for keep in parts:
            way = WAYS[keep][0]
            ty[order, way, 0] = t_push(0, e, t_part[keep], me.at_y(way))
        for keep in parts:
            way = WAYS[1 - keep][0]
            ty[order, way, 1] = t_push(0, e, t_part[keep], me.at_y(way))
            tc[order, 0].append(t_push(0, e, t_part[keep], me.sibling()))

    own_here()
    ax, ar, axf, az, azf = {}, {}, {}, {}, []
    bz, bzf, bx, br, bxf = {}, [], {}, {}, {}
    for way, back, keep in WAYS:
        ar[way] = wire.start(S.at[me.t, a_part[keep]], relay_a.at[keep], me.at_x(way))
    t_spread(0, own, (0, 1))
    for way, back, keep in WAYS:
        ax[way] = wire.start(stu_other.at[A], S.at[me.t, A], me.at_x(way))
    tp = [t_push(0, own, t_part[0], me.partner())]

    def turn_a(dx):
        for way, back, keep in WAYS:
            az[dx, way, 0] = push(piece(0, dx, a_part[keep]), me.at_z(way))
        for way, back, keep in WAYS:
            az[dx, way, 1] = push(piece(0, dx, a_part[1 - keep]), me.at_z(way))

    def turn_b(dz):
        for way, back, keep in WAYS:
            br[dz, way] = wire.start(
                piece(dz, 0, b_part[keep]), relay_b.at[me.zi(dz), keep], me.at_x(way)
            )
        for way in (UP, DOWN):
            bx[dz, way] = wire.start(X.at[me.zi(dz)], piece(dz, 0, B), me.at_x(way))

    turn_a(0)
    own_squares(me, T, part_sq)
    squares = tell(wire, part_sq, me.col_slot, 16, me.at_col)
    for way in (UP, DOWN):
        bz[way] = (push(piece(0, 0, B), me.at_z(way)), push(X.at[me.z], me.at_z(way)))

    for way, back, keep in WAYS:
        ar[way].wait_recv()
        axf[way] = wire.start(relay_a.at[keep], piece(0, back, a_part[keep]), me.at_x(way))
    for way, back, keep in WAYS:
        ax[way].wait_recv()
        turn_a(back)
    tp.append(t_push(0, own, t_part[1], me.partner()))

    def t_far(order, e, keep):
        way, back, _ = WAYS[keep]
        ty[order, way, 0].wait_recv()
        tyf[order].append(t_push(back, e, t_part[keep], me.at_y(way)))

    def t_whole(order, e):
        for way, back, keep in WAYS:
            ty[order, way, 1].wait_recv()
            tc[order, back].append(t_push(back, e, pl.ds(0, PIECE), me.sibling()))

    def t_last(order, e):
        for keep, copy in enumerate(tyf[order]):
            copy.wait_recv()
            tc[order, 2].append(t_push(2, e, t_part[keep], me.sibling()))

    for way, back, keep in WAYS:
        for copy in bz[way]:
            copy.wait_recv()
        bzf.append(push(piece(back, 0, b_part[keep]), me.at_z(way)))
        bzf.append(push(X.at[me.zi(back), x_part[keep]], me.at_z(way)))
    for copy in axf.values():
        copy.wait_recv()
    turn_a(2)
    tp[0].wait_recv()
    t_spread(1, other, (0,))
    t_far(0, own, 0)
    t_far(0, own, 1)
    t_whole(0, own)
    tp[1].wait_recv()
    t_spread(1, other, (1,))
    turn_b(0)
    turn_b(DOWN)
    turn_b(UP)
    for copy in bzf:
        copy.wait_recv()
    turn_b(2)

    def b_relay(dz):
        bxf[dz] = []
        for way, back, keep in WAYS:
            br[dz, way].wait_recv()
            bxf[dz].append(
                wire.start(relay_b.at[me.zi(dz), keep], piece(dz, back, b_part[keep]), me.at_x(way))
            )

    def a_relay(dx):
        for way, back, keep in WAYS:
            az[dx, way, 0].wait_recv()
            azf.append(push(piece(back, dx, a_part[keep]), me.at_z(way)))

    def b_here(dz):
        for way in (UP, DOWN):
            bx[dz, way].wait_recv()
        for copy in bxf[dz]:
            copy.wait_recv()

    def t_here(order, *places):
        for d in places:
            for copy in tc[order, d]:
                copy.wait_recv()

    def a_here(*places):
        for dx in places:
            for way in (UP, DOWN):
                az[dx, way, 1].wait_recv()

    a_relay(0)
    t_last(0, own)
    a_relay(DOWN)
    a_relay(UP)
    t_far(1, other, 0)
    b_relay(0)
    b_relay(DOWN)
    b_relay(UP)
    t_here(0, 0, UP, DOWN, 2)
    b_here(0)
    a_relay(2)
    t_far(1, other, 1)
    cost([me.zi(0)], own, first=True)
    b_relay(2)
    t_whole(1, other)
    a_here(0, UP, DOWN, 2)
    b_here(DOWN)
    b_here(UP)
    cost([me.zi(DOWN), me.zi(UP)], own)
    for copy in azf + squares:
        copy.wait_recv()
    for e in range(2):
        ysq_row[e * PIECE // LANES:(e + 1) * PIECE // LANES, :] = total_of(
            [part_sq[2 * i + e] for i in range(8)]
        )
    b_here(2)
    cost([me.zi(2)], own, last=True, new_rows=True)
    t_last(1, other)
    t_here(1, 0, UP, DOWN)
    cost([me.yi(0), me.yi(DOWN), me.yi(UP)], other, first=True)
    t_here(1, 2)
    cost([me.yi(2)], other, last=True)


def own_squares(me, T, part_sq):
    def block(b, carry):
        rows = aligned(b * LANES, LANES)
        squared = total_of([
            jnp.square(T[me.s, me.h, rows, side * LANES:(side + 1) * LANES].astype(f32))
            for side in range(2)
        ])
        part_sq[me.col_slot, pl.ds(b, 1), :] = jnp.sum(squared.T, axis=0, keepdims=True)
        return carry

    lax.fori_loop(0, PIECE // LANES, block, 0)


def cost_of(me, band, S, T, z, xsq, ysq_row):
    scale = kappa / D

    def cost(groups, e, first=False, last=False, new_rows=False):
        def cols_block(n, carry):
            cols = aligned(n * 256, 256)
            rhs = jnp.concatenate(
                [T[2 * group + i, e, cols, :] for group in groups for i in range(2)], axis=1
            )
            lhs = jnp.concatenate(
                [S[4 * group + i] for group in groups for i in range(4)], axis=1
            )
            prod = lax.dot_general(
                lhs, rhs, (((1,), (1,)), ((), ())), preferred_element_type=f32
            )
            for side in range(2):
                at = e * (TILES // 2) + 2 * n + side
                block = me.row_slot * 4 + e * 2 + lax.div(n, 2)
                for half in range(2):
                    rows = pl.ds(half * BLK, BLK)
                    tile = prod[half * BLK:(half + 1) * BLK, side * LANES:(side + 1) * LANES]
                    tile = tile if first else z[at, rows, :] + tile
                    if last:
                        lowest = band[me.s * 4 + me.h * 2 + half]
                        lowest = jnp.full((BLK, LANES), lowest, jnp.int32)
                        here = jnp.full((BLK, LANES), block, jnp.int32)
                        listed = (here >= lowest) & (here < lowest + W)
                        tile = (2.0 * tile - xsq[rows, :] - ysq_row[pl.ds(at, 1), :]) * scale
                        tile = jnp.where(listed, tile, unlisted)
                    z[at, rows, :] = tile
            return carry

        def squares_block(b, carry):
            rows = aligned(b * LANES, LANES)
            squared = total_of([jnp.square(S[i, rows, :].astype(f32)) for i in range(16)])
            xsq[rows, :] = jnp.broadcast_to(
                jnp.sum(squared, axis=1, keepdims=True), (LANES, LANES)
            )
            return carry

        if new_rows:
            lax.fori_loop(0, LINES, squares_block, 0)
        lax.fori_loop(0, PIECE // 256, cols_block, 0)

    return cost


def spread_lines(compact, tall):
    for c in range(TILES):
        tall[c] = jnp.broadcast_to(compact[c:c + 1, :], (8, LANES))


def row_stats(z, tall, half, lane_high, lane_total, put):
    def lanes(b, carry):
        for part in range(4):
            rows = aligned(b * 64 + part * 16, 16)
            scores = [z[c, rows, :].reshape(2, 8, LANES) + tall[c][None] for c in range(TILES)]
            high = functools.reduce(jnp.maximum, scores)
            lane_high[rows, :] = high.reshape(16, LANES)
            lane_total[rows, :] = total_of([jnp.exp2(v - high) for v in scores]).reshape(16, LANES)
        return carry

    lax.fori_loop(half * (ROWS // 128), (half + 1) * (ROWS // 128), lanes, 0)

    def block(b, carry):
        rows = aligned((half * (LINES // 2) + b) * LANES, LANES)
        value = (lane_high[rows, :] + jnp.log(lane_total[rows, :]) * log2e).T
        top = jnp.max(value, axis=0, keepdims=True)
        total = jnp.sum(jnp.exp2(value - top), axis=0, keepdims=True)
        put(b, top + jnp.log(total) * log2e)
        return carry

    lax.fori_loop(0, LINES // 2, block, 0, unroll=True)


def spread_rows(compact, wide, first=0, count=LINES):
    for b in range(first, first + count):
        line = jnp.broadcast_to(compact[b:b + 1, :], (LANES, LANES))
        wide[b * LANES:(b + 1) * LANES, :] = line.T


def col_stats(z, wide, half, kept, put):
    def tiles(cc, carry):
        if half == 0:
            highs = [jnp.full((8, LANES), unlisted, f32) for _ in range(4)]
            totals = [jnp.zeros((8, LANES), f32) for _ in range(4)]
        else:
            highs = [kept[0, cc * 4 + k] for k in range(4)]
            totals = [kept[1, cc * 4 + k] for k in range(4)]
        for b in range(ROWS // 128):
            rows = pl.ds(half * (ROWS // 2) + b * 64, 64)
            pot = wide[rows, :]
            for k in range(4):
                scores = (z[cc * 4 + k, rows, :] + pot).reshape(8, 8, LANES)
                new = jnp.maximum(highs[k], jnp.max(scores, axis=0))
                totals[k] = totals[k] * jnp.exp2(highs[k] - new) + jnp.sum(
                    jnp.exp2(scores - new[None]), axis=0
                )
                highs[k] = new
        for k in range(4):
            if half == 0:
                kept[0, cc * 4 + k] = highs[k]
                kept[1, cc * 4 + k] = totals[k]
                continue
            top = jnp.max(highs[k], axis=0, keepdims=True)
            total = jnp.sum(totals[k] * jnp.exp2(highs[k] - top), axis=0, keepdims=True)
            put(cc * 4 + k, top + jnp.log(total) * log2e)
        return carry

    lax.fori_loop(0, TILES // 4, tiles, 0)


def tell(wire, slots, index, count, peer):
    return [wire.start(slots.at[index], slots.at[index], peer(d)) for d in range(1, count)]


def swap(wire, slots, index, count, peer):
    for copy in tell(wire, slots, index, count, peer):
        copy.wait_recv()


def sweeps(me, wire, z, wide, stu, tea, tall, row_l, col_l, kept, lane_high, lane_total):
    tea[...] = jnp.zeros_like(tea)
    for sweep in range(ITERS):
        spread_lines(tea, tall)
        rows_sent = []
        for half in range(2):
            rl = row_l.at[sweep, half]

            def put_row(b, value):
                rl[me.row_slot, pl.ds(b, 1), :] = value

            row_stats(z, tall, half, lane_high, lane_total, put_row)
            rows_sent.append(tell(wire, rl, me.row_slot, 8, me.at_row))
        cl = col_l.at[sweep]

        def put_col(c, value):
            cl[me.col_slot, pl.ds(c, 1), :] = value

        for half in range(2):
            rl = row_l.at[sweep, half]
            for copy in rows_sent[half]:
                copy.wait_recv()
            first = half * (LINES // 2)
            stu[first:first + LINES // 2, :] = -log2_tokens - merge([rl[i] for i in range(8)])
            spread_rows(stu, wide, first, LINES // 2)
            col_stats(z, wide, half, kept, put_col)
        swap(wire, cl, me.col_slot, 16, me.at_col)
        tea[...] = -log2_tokens - merge([cl[i] for i in range(16)])


def make_plan(me, z, wide, tall, xsq, ysq_tall, w, sum_r, lane_mass, lane_pull):
    def lanes(b, loss):
        for part in range(4):
            rows = aligned(b * 64 + part * 16, 16)
            pot = (wide[rows, :] + log2_tokens).reshape(2, 8, LANES)
            mass, pull = [], []
            for c in range(TILES):
                tile = z[c, rows, :].reshape(2, 8, LANES)
                scaled = jnp.exp2(tile + pot + tall[c][None])
                loss = loss + total_of([scaled[i] * tile[i] for i in range(2)])
                rounded = scaled.reshape(16, LANES).astype(bf16)
                w[rows, c * LANES:(c + 1) * LANES] = rounded
                rounded = rounded.astype(f32).reshape(2, 8, LANES)
                mass.append(rounded)
                pull.append(rounded * (ysq_tall[c][None] + (D / kappa) * tile))
            lane_mass[rows, :] = total_of(mass).reshape(16, LANES)
            lane_pull[rows, :] = total_of(pull).reshape(16, LANES)
        return loss

    loss = lax.fori_loop(0, ROWS // 64, lanes, jnp.zeros((8, LANES), f32))

    def block(b, carry):
        rows = aligned(b * LANES, LANES)
        mass = jnp.sum(lane_mass[rows, :].T, axis=0, keepdims=True)
        pull = jnp.sum(lane_pull[rows, :].T, axis=0, keepdims=True)
        own = xsq[rows, :].T[0:1, :]
        usable = own > 1e-20
        gamma = jnp.where(usable, 0.5 * (mass + pull / jnp.where(usable, own, 1.0)), 0.0)
        wide[rows, :] = jnp.broadcast_to(gamma, (LANES, LANES)).T
        sum_r[me.row_slot, pl.ds(b, 1), :] = mass - gamma
        return carry

    lax.fori_loop(0, LINES, block, 0, unroll=True)
    sum_r[me.row_slot, LINES:LINES + 8, :] = loss


def pull_of(S, T, w, wide, G):
    def pull(q, part):
        def rows_block(rows):
            prod = jnp.dot(
                w[rows, :], T[q].reshape(COLS, 2 * LANES), preferred_element_type=f32
            )
            gamma = wide[rows, :]
            for side in range(2):
                own = S[2 * q + side, rows, :].astype(f32)
                G[2 * q + side, rows, :] = gamma * own - prod[:, side * LANES:(side + 1) * LANES]

        if part == 0:
            def block(r, carry):
                rows_block(aligned(r * (QA // 2), QA // 2))
                return carry

            lax.fori_loop(0, 2, block, 0)
        else:
            rows_block(pl.ds(QA, QB))

    return pull


def add(dst, terms):
    def block(r, carry):
        rows = aligned(r * 64, 64)
        dst[rows, :] = total_of([term[rows, :].astype(f32) for term in terms]).astype(dst.dtype)
        return carry

    lax.fori_loop(0, dst.shape[0] // 64, block, 0)


def in_two(rows):
    return (pl.ds(0, rows // 2), pl.ds(rows // 2, rows // 2))


def reduce_a(me, wire, G, pull, far_out, near_out, far_in, near_in, x_out, x_in, x_relay, x_far):
    PARTS = in_two(QA)

    def value(t):
        return G.at[t, pl.ds(0, QA)]

    def pull_to(dz):
        for k in range(2):
            pull(2 * me.zi(dz) + k, 0)

    pull_to(2)
    far = []
    for j in range(4):
        add(far_out.at[j], [value(me.zi(2) * 4 + j)])
        far.append([
            wire.start(far_out.at[j, PARTS[keep]], far_in.at[j, keep], me.at_z(way))
            for way, back, keep in WAYS
        ])
    yield
    pull_to(UP)
    pull_to(DOWN)
    near = []
    for j in range(4):
        for way, back, keep in WAYS:
            far[j][keep].wait_recv()
            chained, direct = PARTS[keep], PARTS[1 - keep]
            mine = value(me.zi(way) * 4 + j)
            out = near_out.at[keep, j]
            add(out.at[chained], [mine.at[chained], far_in.at[j, keep]])
            add(out.at[direct], [mine.at[direct]])
            near.append(wire.start(out, near_in.at[keep, j], me.at_z(way)))
    yield
    pull_to(0)
    for copy in near:
        copy.wait_recv()
    for j in range(4):
        mine = value(me.z * 4 + j)
        add(mine, [mine, near_in.at[0, j], near_in.at[1, j]])
    add(x_out.at[2], [value(me.tea(0, 2))])
    far = [
        wire.start(x_out.at[2, PARTS[keep]], x_relay.at[keep], me.at_x(way))
        for way, back, keep in WAYS
    ]
    near = []
    for way, back, keep in WAYS:
        add(x_out.at[keep], [value(me.tea(0, way))])
        near.append(wire.start(x_out.at[keep], x_in.at[keep], me.at_x(way)))
    yield
    last = []
    for way, back, keep in WAYS:
        far[keep].wait_recv()
        last.append(wire.start(x_relay.at[keep], x_far.at[PARTS[keep]], me.at_x(way)))
    yield
    for copy in near + last:
        copy.wait_recv()
    yield


def reduce_b(
    me, wire, G, pull, far_out, relay, x_out, x_in, x_far, others,
    z_far_out, z_far_in, z_out, z_in,
):
    PARTS = in_two(QB)
    order = (2, UP, DOWN, 0)

    def value(t):
        return G.at[t, pl.ds(QA, QB)]

    far, near, last = {}, {}, {}
    for dz in order:
        pull(2 * me.zi(dz) + 1 - me.l, 1)
        add(far_out.at[me.zi(dz)], [value(me.tea(dz, 2))])
        far[dz] = [
            wire.start(
                far_out.at[me.zi(dz), PARTS[keep]], relay.at[me.zi(dz), keep], me.at_x(way)
            )
            for way, back, keep in WAYS
        ]
    yield
    for dz in order:
        pull(2 * me.zi(dz) + me.l, 1)
        near[dz] = []
        for way, back, keep in WAYS:
            add(x_out.at[keep, me.zi(dz)], [value(me.tea(dz, way))])
            near[dz].append(
                wire.start(x_out.at[keep, me.zi(dz)], x_in.at[keep, me.zi(dz)], me.at_x(way))
            )
        last[dz] = []
        for way, back, keep in WAYS:
            far[dz][keep].wait_recv()
            last[dz].append(
                wire.start(relay.at[me.zi(dz), keep], x_far.at[me.zi(dz), PARTS[keep]], me.at_x(way))
            )
    yield

    def arrived(dz):
        for copy in near[dz] + last[dz]:
            copy.wait_recv()
        mine, other = value(me.tea(dz, 0)), others.at[me.zi(dz)]
        add(mine, [mine, x_far.at[me.zi(dz)]])
        add(other, [x_in.at[0, me.zi(dz)], x_in.at[1, me.zi(dz)]])
        return mine, other

    z_far = {}
    for i, term in enumerate(arrived(2)):
        add(z_far_out.at[i], [term])
        for way, back, keep in WAYS:
            z_far[i, way] = wire.start(
                z_far_out.at[i, PARTS[keep]], z_far_in.at[i, keep], me.at_z(way)
            )
    yield
    z_near = []
    terms = {way: arrived(way) for way in (UP, DOWN)}
    for i in range(2):
        for way, back, keep in WAYS:
            z_far[i, way].wait_recv()
            chained, direct = PARTS[keep], PARTS[1 - keep]
            term, out = terms[way][i], z_out.at[i, keep]
            add(out.at[chained], [term.at[chained], z_far_in.at[i, keep]])
            add(out.at[direct], [term.at[direct]])
            z_near.append(wire.start(out, z_in.at[i, keep], me.at_z(way)))
    yield
    terms = arrived(0)
    for copy in z_near:
        copy.wait_recv()
    for i, term in enumerate(terms):
        add(term, [term, z_in.at[i, 0], z_in.at[i, 1]])
    yield


def kernel(
    band, stu_in, tea_in, grad_out, stu_out, tea_out, loss,
    S, T, X, stu_other, grad, relay_a, relay_b, z, w, G, wide, xsq, xsq_other, part_sq, ysq_row, stu, tea, tall, ysq_tall,
    kept, row_l, col_l, sum_r, sum_c, pair_f, pair_b, others,
    a_far_out, a_near_out, a_far_in, a_near_in, a_x_out, a_x_in, a_x_relay, a_x_far,
    b_far_out, b_relay, b_x_out, b_x_in, b_x_far, b_z_far_out, b_z_far_in, b_z_out, b_z_in,
    send, recv, here,
):
    me = Place()
    mine = pl.multiple_of(me.h * ROWS, ROWS)
    other = pl.multiple_of((1 - me.h) * ROWS, ROWS)
    loads = [
        pltpu.make_async_copy(tea_in, T.at[me.s, me.h], here.at[0]),
        pltpu.make_async_copy(stu_in.at[pl.ds(mine, ROWS)], S.at[me.t], here.at[1]),
        pltpu.make_async_copy(stu_in.at[pl.ds(other, ROWS)], stu_other, here.at[2]),
        pltpu.make_async_copy(stu_in.at[pl.ds(other + GA, GB)], X.at[me.z], here.at[3]),
    ]
    for copy in loads:
        copy.start()
    barrier = pltpu.get_barrier_semaphore()
    peers = [me.outer()] + [me.at_row(d) for d in range(1, 8)] + [me.at_col(d) for d in range(1, 16)]
    for peer in peers:
        pl.semaphore_signal(barrier, inc=1, device_id=peer, device_id_type=MESH)

    def own_here():
        for copy in loads:
            copy.wait()
        pl.semaphore_wait(barrier, len(peers))

    wire = Wire(send, recv)
    gather(
        me, wire, stu_other, own_here, S, T, X, relay_a, relay_b, part_sq, ysq_row,
        cost_of(me, band, S, T, z, xsq, ysq_row),
    )
    sweeps(me, wire, z, wide, stu, tea, tall, row_l, col_l, kept, G.at[0], G.at[1])
    spread_lines(tea, tall)
    spread_lines(ysq_row, ysq_tall)
    make_plan(me, z, wide, tall, xsq, ysq_tall, w, sum_r, G.at[0], G.at[1])
    sums = tell(wire, sum_r, me.row_slot, 8, me.at_row)
    pair_f[me.h] = stu[...] / kappa
    sums.append(wire.start(pair_f.at[me.h], pair_f.at[me.h], me.partner()))
    tea[...] = tea[...] / kappa
    stores = [
        pltpu.make_async_copy(tea.at[aligned(me.h * LINES, LINES)], tea_out, here.at[4])
    ]
    stores[-1].start()
    pull = pull_of(S, T, w, wide, G)
    first = reduce_a(
        me, wire, G, pull, a_far_out, a_near_out, a_far_in, a_near_in,
        a_x_out, a_x_in, a_x_relay, a_x_far,
    )
    second = reduce_b(
        me, wire, G, pull, b_far_out, b_relay, b_x_out, b_x_in, b_x_far, others,
        b_z_far_out, b_z_far_in, b_z_out, b_z_in,
    )
    steps = [first, second] * 3 + [second, first, second, first]
    for number, step in enumerate(steps):
        next(step)
        if number == 1:
            for copy in sums:
                copy.wait_recv()
            summed = total_of([sum_r[i] for i in range(8)])
            sum_c[me.col_slot] = summed[LINES:, :]
            pair_b[me.h] = summed[:LINES, :]
            sums = tell(wire, sum_c, me.col_slot, 16, me.at_col)
            sums.append(wire.start(pair_b.at[me.h], pair_b.at[me.h], me.partner()))
            stores.append(pltpu.make_async_copy(pair_f, stu_out, here.at[5]))
            stores[-1].start()
        if number == 3:
            for copy in sums:
                copy.wait_recv()
            total = total_of([sum_c[i] for i in range(16)])
            total = jnp.sum(jnp.sum(total, axis=0, keepdims=True), axis=1, keepdims=True)
            loss[...] = total * (-1.0 / (kappa * TOKENS))
            spread_rows(pair_b.at[me.h], xsq)
            spread_rows(pair_b.at[1 - me.h], xsq_other)

    def finish(first_row, rows_total, own_terms, other_terms, at):
        def block(r, carry):
            near = aligned(r * LANES, LANES)
            rows = aligned(first_row + r * LANES, LANES)
            grad[aligned(mine + first_row + r * LANES, LANES), :] = (
                xsq[rows, :] * S[me.t, rows, :].astype(f32)
                + total_of([term[near, :].astype(f32) for term in own_terms])
            )
            grad[aligned(other + first_row + r * LANES, LANES), :] = (
                xsq_other[rows, :] * stu_other[rows, :].astype(f32)
                + total_of([term[near, :].astype(f32) for term in other_terms])
            )
            return carry

        lax.fori_loop(0, rows_total // LANES, block, 0)
        for i, base in enumerate((mine, other)):
            rows = aligned(base + first_row, LANES)
            rows = pl.ds(rows.start, rows_total)
            stores.append(
                pltpu.make_async_copy(grad.at[rows], grad_out.at[rows], here.at[at + i])
            )
            stores[-1].start()

    finish(0, QA, [G.at[me.t, pl.ds(0, QA)], a_x_far], [a_x_in.at[0], a_x_in.at[1]], 6)
    finish(QA, QB, [G.at[me.t, pl.ds(QA, QB)]], [others.at[me.z]], 8)
    assert wire.used <= WIRES, wire.used
    wire.drain()
    for copy in stores:
        copy.wait()


def one_device(band_start, student, teacher):
    dma = pltpu.SemaphoreType.DMA
    vmem = pl.BlockSpec(memory_space=pltpu.VMEM)
    anywhere = pl.BlockSpec(memory_space=pl.ANY)

    def wide_bf16(*lead):
        return pltpu.VMEM((*lead, LANES), bf16)

    def wide_f32(*lead):
        return pltpu.VMEM((*lead, LANES), f32)

    scratch = [
        wide_bf16(16, ROWS),
        pltpu.VMEM((8, 2, PIECE, 2 * LANES), bf16),
        wide_bf16(4, GB),
        wide_bf16(ROWS),
        wide_f32(OWNED),
        wide_bf16(2, GA // 2),
        wide_bf16(4, 2, GB // 2),
        wide_f32(TILES, ROWS),
        pltpu.VMEM((ROWS, COLS), bf16),
        wide_f32(16, ROWS),
        wide_f32(ROWS),
        wide_f32(ROWS),
        wide_f32(ROWS),
        wide_f32(16, PIECE // LANES),
        wide_f32(TILES),
        wide_f32(LINES),
        wide_f32(TILES),
        wide_f32(TILES, 8),
        wide_f32(TILES, 8),
        wide_f32(2, TILES, 8),
        wide_f32(ITERS, 2, 8, LINES // 2),
        wide_f32(ITERS, 16, TILES),
        wide_f32(8, LINES + 8),
        wide_f32(16, 8),
        wide_f32(2, LINES),
        wide_f32(2, LINES),
        wide_f32(4, QB),
        wide_bf16(4, QA), wide_bf16(2, 4, QA), wide_bf16(4, 2, QA // 2), wide_bf16(2, 4, QA),
        wide_bf16(3, QA), wide_bf16(2, QA), wide_bf16(2, QA // 2), wide_bf16(QA),
        wide_bf16(4, QB), wide_bf16(4, 2, QB // 2), wide_bf16(2, 4, QB), wide_bf16(2, 4, QB),
        wide_bf16(4, QB),
        wide_bf16(2, QB), wide_bf16(2, 2, QB // 2), wide_bf16(2, 2, QB), wide_bf16(2, 2, QB),
        dma((WIRES,)),
        dma((WIRES,)),
        dma((10,)),
    ]
    return pl.pallas_call(
        kernel,
        out_shape=(
            jax.ShapeDtypeStruct((OWNED, LANES), f32),
            jax.ShapeDtypeStruct((2, LINES, LANES), f32),
            jax.ShapeDtypeStruct((LINES, LANES), f32),
            jax.ShapeDtypeStruct((1, 1), f32),
        ),
        in_specs=[pl.BlockSpec(memory_space=pltpu.SMEM), anywhere, anywhere],
        out_specs=(anywhere, anywhere, anywhere, vmem),
        scratch_shapes=scratch,
        compiler_params=pltpu.CompilerParams(
            collective_id=0, has_side_effects=True, vmem_limit_bytes=62 * 2**20
        ),
    )(band_start, student, teacher)


def local(student, teacher, band_start):
    grad, stu, tea, loss = one_device(band_start, student, teacher)
    return (grad, stu.reshape(OWNED), tea.reshape(PIECE), loss.reshape(()))


def solution(mesh):
    placed = (P("stu", "tea"), P("tea", "stu"), P())
    return jax.shard_map(
        local,
        mesh=mesh,
        in_specs=placed,
        out_specs=(P("stu", "tea"), P("stu"), P("tea"), P()),
        check_vma=False,
    )
```

```python
import functools
import math

import jax
import jax.numpy as jnp
from jax import lax
from jax.experimental import pallas as pl
from jax.experimental.pallas import tpu as pltpu
from jax.sharding import PartitionSpec as P

D = 2048
BLK = 512
W = 4
ITERS = 3
LANES = 128
OWNED = 2048
ROWS = 1024
COLS = 2048
PIECE = 1024
TILES = COLS // LANES
LINES = ROWS // LANES
TOKENS = 16384
GA, GB = 768, 256
QA, QB = 576, 448
WIRES = 300
UP, DOWN = 1, 3

epsilon = 0.02
kappa = math.log2(math.e) / epsilon
log2e = math.log2(math.e)
log2_tokens = math.log2(TOKENS)
unlisted = -1e30
MESH = pl.DeviceIdType.MESH
f32 = jnp.float32
bf16 = jnp.bfloat16


def aligned(start, size):
    return pl.ds(pl.multiple_of(start, size), size)


def total_of(parts):
    return functools.reduce(lambda a, b: a + b, parts)


def merge(parts):
    highest = functools.reduce(jnp.maximum, parts)
    return highest + jnp.log(total_of([jnp.exp2(p - highest) for p in parts])) * log2e


class Place:
    def __init__(self):
        self.s = lax.axis_index("stu")
        self.t = lax.axis_index("tea")
        self.y = lax.div(self.s, 2)
        self.core = lax.rem(self.s, 2)
        self.z = lax.div(self.t, 4)
        self.x = lax.rem(self.t, 4)
        self.h = lax.rem(self.x, 2)
        self.l = lax.div(self.x, 2)
        self.row_slot = 2 * self.z + self.l
        self.col_slot = 2 * self.s + self.h

    def zi(self, dz):
        return lax.rem(self.z + dz, 4)

    def yi(self, dy):
        return lax.rem(self.y + dy, 4)

    def xi(self, dx):
        return lax.rem(self.x + dx, 4)

    def tea(self, dz, dx):
        return self.zi(dz) * 4 + self.xi(dx)

    def stu(self, dy):
        return lax.rem(self.y + dy, 4) * 2 + self.core

    def at_x(self, d):
        return (self.s, self.tea(0, d))

    def at_z(self, d):
        return (self.s, self.tea(d, 0))

    def at_y(self, d):
        return (self.stu(d), self.t)

    def sibling(self):
        return (self.y * 2 + 1 - self.core, self.t)

    def partner(self):
        return (self.s, self.z * 4 + self.l * 2 + 1 - self.h)

    def outer(self):
        return (self.s, self.z * 4 + lax.rem(self.x + 3 + 2 * self.h, 4))

    def at_row(self, d):
        k = lax.rem(self.row_slot + d, 8)
        return (self.s, lax.div(k, 2) * 4 + lax.rem(k, 2) * 2 + self.h)

    def at_col(self, d):
        k = lax.rem(self.col_slot + d, 16)
        return (lax.div(k, 2), self.z * 4 + self.l * 2 + lax.rem(k, 2))


class Wire:
    def __init__(self, send, recv):
        self.send, self.recv, self.used, self.open = send, recv, 0, []

    def start(self, src, dst, device):
        copy = pltpu.make_async_remote_copy(
            src_ref=src, dst_ref=dst,
            send_sem=self.send.at[self.used], recv_sem=self.recv.at[self.used],
            device_id=device, device_id_type=MESH,
        )
        self.used += 1
        copy.start()
        self.open.append(copy)
        return copy

    def drain(self):
        for copy in self.open:
            copy.wait_send()
        self.open = []


WAYS = ((UP, DOWN, 0), (DOWN, UP, 1))


def gather(me, wire, stu_other, own_here, S, T, X, relay_a, relay_b, part_sq, ysq_row, cost):
    A, B = pl.ds(0, GA), pl.ds(GA, GB)
    a_part = [pl.ds(0, GA // 2), pl.ds(GA // 2, GA // 2)]
    b_part = [pl.ds(GA, GB // 2), pl.ds(GA + GB // 2, GB // 2)]
    x_part = [pl.ds(0, GB // 2), pl.ds(GB // 2, GB // 2)]
    t_part = [pl.ds(0, PIECE // 2), pl.ds(PIECE // 2, PIECE // 2)]

    def push(ref, device):
        return wire.start(ref, ref, device)

    def piece(dz, dx, rows):
        return S.at[me.tea(dz, dx), rows]

    def t_push(dy, e, rows, device):
        return push(T.at[me.stu(dy), e, rows], device)

    own, other = me.h, 1 - me.h
    ty, tyf = {}, {0: [], 1: []}
    tc = {(order, d): [] for order in range(2) for d in (0, UP, DOWN, 2)}

    def t_spread(order, e, parts):
        for keep in parts:
            way = WAYS[keep][0]
            ty[order, way, 0] = t_push(0, e, t_part[keep], me.at_y(way))
        for keep in parts:
            way = WAYS[1 - keep][0]
            ty[order, way, 1] = t_push(0, e, t_part[keep], me.at_y(way))
            tc[order, 0].append(t_push(0, e, t_part[keep], me.sibling()))

    own_here()
    ax, ar, axf, az, azf = {}, {}, {}, {}, []
    bz, bzf, bx, br, bxf = {}, [], {}, {}, {}
    for way, back, keep in WAYS:
        ar[way] = wire.start(S.at[me.t, a_part[keep]], relay_a.at[keep], me.at_x(way))
    t_spread(0, own, (0, 1))
    for way, back, keep in WAYS:
        ax[way] = wire.start(stu_other.at[A], S.at[me.t, A], me.at_x(way))
    tp = [t_push(0, own, t_part[0], me.partner())]

    def turn_a(dx):
        for way, back, keep in WAYS:
            az[dx, way, 0] = push(piece(0, dx, a_part[keep]), me.at_z(way))
        for way, back, keep in WAYS:
            az[dx, way, 1] = push(piece(0, dx, a_part[1 - keep]), me.at_z(way))

    def turn_b(dz):
        for way, back, keep in WAYS:
            br[dz, way] = wire.start(
                piece(dz, 0, b_part[keep]), relay_b.at[me.zi(dz), keep], me.at_x(way)
            )
        for way in (UP, DOWN):
            bx[dz, way] = wire.start(X.at[me.zi(dz)], piece(dz, 0, B), me.at_x(way))

    turn_a(0)
    own_squares(me, T, part_sq)
    squares = tell(wire, part_sq, me.col_slot, 16, me.at_col)
    for way in (UP, DOWN):
        bz[way] = (push(piece(0, 0, B), me.at_z(way)), push(X.at[me.z], me.at_z(way)))

    for way, back, keep in WAYS:
        ar[way].wait_recv()
        axf[way] = wire.start(relay_a.at[keep], piece(0, back, a_part[keep]), me.at_x(way))
    for way, back, keep in WAYS:
        ax[way].wait_recv()
        turn_a(back)
    tp.append(t_push(0, own, t_part[1], me.partner()))

    def t_far(order, e, keep):
        way, back, _ = WAYS[keep]
        ty[order, way, 0].wait_recv()
        tyf[order].append(t_push(back, e, t_part[keep], me.at_y(way)))

    def t_whole(order, e):
        for way, back, keep in WAYS:
            ty[order, way, 1].wait_recv()
            tc[order, back].append(t_push(back, e, pl.ds(0, PIECE), me.sibling()))

    def t_last(order, e):
        for keep, copy in enumerate(tyf[order]):
            copy.wait_recv()
            tc[order, 2].append(t_push(2, e, t_part[keep], me.sibling()))

    for way, back, keep in WAYS:
        for copy in bz[way]:
            copy.wait_recv()
        bzf.append(push(piece(back, 0, b_part[keep]), me.at_z(way)))
        bzf.append(push(X.at[me.zi(back), x_part[keep]], me.at_z(way)))
    for copy in axf.values():
        copy.wait_recv()
    turn_a(2)
    tp[0].wait_recv()
    t_spread(1, other, (0,))
    t_far(0, own, 0)
    t_far(0, own, 1)
    t_whole(0, own)
    tp[1].wait_recv()
    t_spread(1, other, (1,))
    turn_b(0)
    turn_b(DOWN)
    turn_b(UP)
    for copy in bzf:
        copy.wait_recv()
    turn_b(2)

    def b_relay(dz):
        bxf[dz] = []
        for way, back, keep in WAYS:
            br[dz, way].wait_recv()
            bxf[dz].append(
                wire.start(relay_b.at[me.zi(dz), keep], piece(dz, back, b_part[keep]), me.at_x(way))
            )

    def a_relay(dx):
        for way, back, keep in WAYS:
            az[dx, way, 0].wait_recv()
            azf.append(push(piece(back, dx, a_part[keep]), me.at_z(way)))

    def b_here(dz):
        for way in (UP, DOWN):
            bx[dz, way].wait_recv()
        for copy in bxf[dz]:
            copy.wait_recv()

    def t_here(order, *places):
        for d in places:
            for copy in tc[order, d]:
                copy.wait_recv()

    def a_here(*places):
        for dx in places:
            for way in (UP, DOWN):
                az[dx, way, 1].wait_recv()

    a_relay(0)
    t_last(0, own)
    a_relay(DOWN)
    a_relay(UP)
    t_far(1, other, 0)
    b_relay(0)
    b_relay(DOWN)
    b_relay(UP)
    t_here(0, 0, UP, DOWN, 2)
    b_here(0)
    a_relay(2)
    t_far(1, other, 1)
    cost([me.zi(0)], own, first=True)
    b_relay(2)
    t_whole(1, other)
    a_here(0, UP, DOWN, 2)
    b_here(DOWN)
    b_here(UP)
    cost([me.zi(DOWN), me.zi(UP)], own)
    for copy in azf + squares:
        copy.wait_recv()
    for e in range(2):
        ysq_row[e * PIECE // LANES:(e + 1) * PIECE // LANES, :] = total_of(
            [part_sq[2 * i + e] for i in range(8)]
        )
    b_here(2)
    cost([me.zi(2)], own, last=True, new_rows=True)
    t_last(1, other)
    t_here(1, 0, UP, DOWN)
    cost([me.yi(0), me.yi(DOWN), me.yi(UP)], other, first=True)
    t_here(1, 2)
    cost([me.yi(2)], other, last=True)


def own_squares(me, T, part_sq):
    def block(b, carry):
        rows = aligned(b * LANES, LANES)
        squared = total_of([
            jnp.square(T[me.s, me.h, rows, side * LANES:(side + 1) * LANES].astype(f32))
            for side in range(2)
        ])
        part_sq[me.col_slot, pl.ds(b, 1), :] = jnp.sum(squared.T, axis=0, keepdims=True)
        return carry

    lax.fori_loop(0, PIECE // LANES, block, 0)


def cost_of(me, band, S, T, z, xsq, ysq_row):
    scale = kappa / D

    def cost(groups, e, first=False, last=False, new_rows=False):
        def cols_block(n, carry):
            cols = aligned(n * 256, 256)
            rhs = jnp.concatenate(
                [T[2 * group + i, e, cols, :] for group in groups for i in range(2)], axis=1
            )
            lhs = jnp.concatenate(
                [S[4 * group + i] for group in groups for i in range(4)], axis=1
            )
            prod = lax.dot_general(
                lhs, rhs, (((1,), (1,)), ((), ())), preferred_element_type=f32
            )
            for side in range(2):
                at = e * (TILES // 2) + 2 * n + side
                block = me.row_slot * 4 + e * 2 + lax.div(n, 2)
                for half in range(2):
                    rows = pl.ds(half * BLK, BLK)
                    tile = prod[half * BLK:(half + 1) * BLK, side * LANES:(side + 1) * LANES]
                    tile = tile if first else z[at, rows, :] + tile
                    if last:
                        lowest = band[me.s * 4 + me.h * 2 + half]
                        lowest = jnp.full((BLK, LANES), lowest, jnp.int32)
                        here = jnp.full((BLK, LANES), block, jnp.int32)
                        listed = (here >= lowest) & (here < lowest + W)
                        tile = (2.0 * tile - xsq[rows, :] - ysq_row[pl.ds(at, 1), :]) * scale
                        tile = jnp.where(listed, tile, unlisted)
                    z[at, rows, :] = tile
            return carry

        def squares_block(b, carry):
            rows = aligned(b * LANES, LANES)
            squared = total_of([jnp.square(S[i, rows, :].astype(f32)) for i in range(16)])
            xsq[rows, :] = jnp.broadcast_to(
                jnp.sum(squared, axis=1, keepdims=True), (LANES, LANES)
            )
            return carry

        if new_rows:
            lax.fori_loop(0, LINES, squares_block, 0)
        lax.fori_loop(0, PIECE // 256, cols_block, 0)

    return cost


def spread_lines(compact, tall):
    for c in range(TILES):
        tall[c] = jnp.broadcast_to(compact[c:c + 1, :], (8, LANES))


def row_stats(z, tall, half, lane_high, lane_total, put):
    def lanes(b, carry):
        for part in range(4):
            rows = aligned(b * 64 + part * 16, 16)
            scores = [z[c, rows, :].reshape(2, 8, LANES) + tall[c][None] for c in range(TILES)]
            high = functools.reduce(jnp.maximum, scores)
            lane_high[rows, :] = high.reshape(16, LANES)
            lane_total[rows, :] = total_of([jnp.exp2(v - high) for v in scores]).reshape(16, LANES)
        return carry

    lax.fori_loop(half * (ROWS // 128), (half + 1) * (ROWS // 128), lanes, 0)

    def block(b, carry):
        rows = aligned((half * (LINES // 2) + b) * LANES, LANES)
        value = (lane_high[rows, :] + jnp.log(lane_total[rows, :]) * log2e).T
        top = jnp.max(value, axis=0, keepdims=True)
        total = jnp.sum(jnp.exp2(value - top), axis=0, keepdims=True)
        put(b, top + jnp.log(total) * log2e)
        return carry

    lax.fori_loop(0, LINES // 2, block, 0, unroll=True)


def spread_rows(compact, wide, first=0, count=LINES):
    for b in range(first, first + count):
        line = jnp.broadcast_to(compact[b:b + 1, :], (LANES, LANES))
        wide[b * LANES:(b + 1) * LANES, :] = line.T


def col_stats(z, wide, half, kept, put):
    def tiles(cc, carry):
        if half == 0:
            highs = [jnp.full((8, LANES), unlisted, f32) for _ in range(4)]
            totals = [jnp.zeros((8, LANES), f32) for _ in range(4)]
        else:
            highs = [kept[0, cc * 4 + k] for k in range(4)]
            totals = [kept[1, cc * 4 + k] for k in range(4)]
        for b in range(ROWS // 128):
            rows = pl.ds(half * (ROWS // 2) + b * 64, 64)
            pot = wide[rows, :]
            for k in range(4):
                scores = (z[cc * 4 + k, rows, :] + pot).reshape(8, 8, LANES)
                new = jnp.maximum(highs[k], jnp.max(scores, axis=0))
                totals[k] = totals[k] * jnp.exp2(highs[k] - new) + jnp.sum(
                    jnp.exp2(scores - new[None]), axis=0
                )
                highs[k] = new
        for k in range(4):
            if half == 0:
                kept[0, cc * 4 + k] = highs[k]
                kept[1, cc * 4 + k] = totals[k]
                continue
            top = jnp.max(highs[k], axis=0, keepdims=True)
            total = jnp.sum(totals[k] * jnp.exp2(highs[k] - top), axis=0, keepdims=True)
            put(cc * 4 + k, top + jnp.log(total) * log2e)
        return carry

    lax.fori_loop(0, TILES // 4, tiles, 0)


def tell(wire, slots, index, count, peer):
    return [wire.start(slots.at[index], slots.at[index], peer(d)) for d in range(1, count)]


def swap(wire, slots, index, count, peer):
    for copy in tell(wire, slots, index, count, peer):
        copy.wait_recv()


def sweeps(me, wire, z, wide, stu, tea, tall, row_l, col_l, kept, lane_high, lane_total):
    tea[...] = jnp.zeros_like(tea)
    for sweep in range(ITERS):
        spread_lines(tea, tall)
        rows_sent = []
        for half in range(2):
            rl = row_l.at[sweep, half]

            def put_row(b, value):
                rl[me.row_slot, pl.ds(b, 1), :] = value

            row_stats(z, tall, half, lane_high, lane_total, put_row)
            rows_sent.append(tell(wire, rl, me.row_slot, 8, me.at_row))
        cl = col_l.at[sweep]

        def put_col(c, value):
            cl[me.col_slot, pl.ds(c, 1), :] = value

        for half in range(2):
            rl = row_l.at[sweep, half]
            for copy in rows_sent[half]:
                copy.wait_recv()
            first = half * (LINES // 2)
            stu[first:first + LINES // 2, :] = -log2_tokens - merge([rl[i] for i in range(8)])
            spread_rows(stu, wide, first, LINES // 2)
            col_stats(z, wide, half, kept, put_col)
        swap(wire, cl, me.col_slot, 16, me.at_col)
        tea[...] = -log2_tokens - merge([cl[i] for i in range(16)])


def make_plan(me, z, wide, tall, xsq, ysq_tall, w, sum_r, lane_mass, lane_pull):
    def lanes(b, loss):
        for part in range(4):
            rows = aligned(b * 64 + part * 16, 16)
            pot = (wide[rows, :] + log2_tokens).reshape(2, 8, LANES)
            mass, pull = [], []
            for c in range(TILES):
                tile = z[c, rows, :].reshape(2, 8, LANES)
                scaled = jnp.exp2(tile + pot + tall[c][None])
                loss = loss + total_of([scaled[i] * tile[i] for i in range(2)])
                rounded = scaled.reshape(16, LANES).astype(bf16)
                w[rows, c * LANES:(c + 1) * LANES] = rounded
                rounded = rounded.astype(f32).reshape(2, 8, LANES)
                mass.append(rounded)
                pull.append(rounded * (ysq_tall[c][None] + (D / kappa) * tile))
            lane_mass[rows, :] = total_of(mass).reshape(16, LANES)
            lane_pull[rows, :] = total_of(pull).reshape(16, LANES)
        return loss

    loss = lax.fori_loop(0, ROWS // 64, lanes, jnp.zeros((8, LANES), f32))

    def block(b, carry):
        rows = aligned(b * LANES, LANES)
        mass = jnp.sum(lane_mass[rows, :].T, axis=0, keepdims=True)
        pull = jnp.sum(lane_pull[rows, :].T, axis=0, keepdims=True)
        own = xsq[rows, :].T[0:1, :]
        usable = own > 1e-20
        gamma = jnp.where(usable, 0.5 * (mass + pull / jnp.where(usable, own, 1.0)), 0.0)
        wide[rows, :] = jnp.broadcast_to(gamma, (LANES, LANES)).T
        sum_r[me.row_slot, pl.ds(b, 1), :] = mass - gamma
        return carry

    lax.fori_loop(0, LINES, block, 0, unroll=True)
    sum_r[me.row_slot, LINES:LINES + 8, :] = loss


def pull_of(S, T, w, wide, G):
    def pull(q, part):
        def rows_block(rows):
            prod = jnp.dot(
                w[rows, :], T[q].reshape(COLS, 2 * LANES), preferred_element_type=f32
            )
            gamma = wide[rows, :]
            for side in range(2):
                own = S[2 * q + side, rows, :].astype(f32)
                G[2 * q + side, rows, :] = gamma * own - prod[:, side * LANES:(side + 1) * LANES]

        if part == 0:
            def block(r, carry):
                rows_block(aligned(r * (QA // 2), QA // 2))
                return carry

            lax.fori_loop(0, 2, block, 0)
        else:
            rows_block(pl.ds(QA, QB))

    return pull


def add(dst, terms):
    size = 96 if dst.shape[0] % 96 == 0 else 112

    def block(r, carry):
        rows = aligned(r * size, size)
        dst[rows, :] = total_of([term[rows, :].astype(f32) for term in terms]).astype(dst.dtype)
        return carry

    lax.fori_loop(0, dst.shape[0] // size, block, 0)


def in_two(rows):
    return (pl.ds(0, rows // 2), pl.ds(rows // 2, rows // 2))


def reduce_a(me, wire, G, pull, far_out, near_out, far_in, near_in, x_out, x_in, x_relay, x_far):
    PARTS = in_two(QA)

    def value(t):
        return G.at[t, pl.ds(0, QA)]

    def pull_to(dz):
        for k in range(2):
            pull(2 * me.zi(dz) + k, 0)

    pull_to(2)
    far = []
    for j in range(4):
        add(far_out.at[j], [value(me.zi(2) * 4 + j)])
        far.append([
            wire.start(far_out.at[j, PARTS[keep]], far_in.at[j, keep], me.at_z(way))
            for way, back, keep in WAYS
        ])
    yield
    pull_to(UP)
    pull_to(DOWN)
    near = []
    for j in range(4):
        for way, back, keep in WAYS:
            far[j][keep].wait_recv()
            chained, direct = PARTS[keep], PARTS[1 - keep]
            mine = value(me.zi(way) * 4 + j)
            out = near_out.at[keep, j]
            add(out.at[chained], [mine.at[chained], far_in.at[j, keep]])
            add(out.at[direct], [mine.at[direct]])
            near.append(wire.start(out, near_in.at[keep, j], me.at_z(way)))
    yield
    pull_to(0)
    for copy in near:
        copy.wait_recv()
    for j in range(4):
        mine = value(me.z * 4 + j)
        add(mine, [mine, near_in.at[0, j], near_in.at[1, j]])
    add(x_out.at[2], [value(me.tea(0, 2))])
    far = [
        wire.start(x_out.at[2, PARTS[keep]], x_relay.at[keep], me.at_x(way))
        for way, back, keep in WAYS
    ]
    near = []
    for way, back, keep in WAYS:
        add(x_out.at[keep], [value(me.tea(0, way))])
        near.append(wire.start(x_out.at[keep], x_in.at[keep], me.at_x(way)))
    yield
    last = []
    for way, back, keep in WAYS:
        far[keep].wait_recv()
        last.append(wire.start(x_relay.at[keep], x_far.at[PARTS[keep]], me.at_x(way)))
    yield
    for copy in near + last:
        copy.wait_recv()
    yield


def reduce_b(
    me, wire, G, pull, far_out, relay, x_out, x_in, x_far, others,
    z_far_out, z_far_in, z_out, z_in,
):
    PARTS = in_two(QB)
    order = (2, UP, DOWN, 0)

    def value(t):
        return G.at[t, pl.ds(QA, QB)]

    far, near, last = {}, {}, {}
    for dz in order:
        pull(2 * me.zi(dz) + 1 - me.l, 1)
        add(far_out.at[me.zi(dz)], [value(me.tea(dz, 2))])
        far[dz] = [
            wire.start(
                far_out.at[me.zi(dz), PARTS[keep]], relay.at[me.zi(dz), keep], me.at_x(way)
            )
            for way, back, keep in WAYS
        ]
    yield
    for dz in order:
        pull(2 * me.zi(dz) + me.l, 1)
        near[dz] = []
        for way, back, keep in WAYS:
            add(x_out.at[keep, me.zi(dz)], [value(me.tea(dz, way))])
            near[dz].append(
                wire.start(x_out.at[keep, me.zi(dz)], x_in.at[keep, me.zi(dz)], me.at_x(way))
            )
        last[dz] = []
        for way, back, keep in WAYS:
            far[dz][keep].wait_recv()
            last[dz].append(
                wire.start(relay.at[me.zi(dz), keep], x_far.at[me.zi(dz), PARTS[keep]], me.at_x(way))
            )
    yield

    def arrived(dz):
        for copy in near[dz] + last[dz]:
            copy.wait_recv()
        mine, other = value(me.tea(dz, 0)), others.at[me.zi(dz)]
        add(mine, [mine, x_far.at[me.zi(dz)]])
        add(other, [x_in.at[0, me.zi(dz)], x_in.at[1, me.zi(dz)]])
        return mine, other

    z_far = {}
    for i, term in enumerate(arrived(2)):
        add(z_far_out.at[i], [term])
        for way, back, keep in WAYS:
            z_far[i, way] = wire.start(
                z_far_out.at[i, PARTS[keep]], z_far_in.at[i, keep], me.at_z(way)
            )
    yield
    z_near = []
    terms = {way: arrived(way) for way in (UP, DOWN)}
    for i in range(2):
        for way, back, keep in WAYS:
            z_far[i, way].wait_recv()
            chained, direct = PARTS[keep], PARTS[1 - keep]
            term, out = terms[way][i], z_out.at[i, keep]
            add(out.at[chained], [term.at[chained], z_far_in.at[i, keep]])
            add(out.at[direct], [term.at[direct]])
            z_near.append(wire.start(out, z_in.at[i, keep], me.at_z(way)))
    yield
    terms = arrived(0)
    for copy in z_near:
        copy.wait_recv()
    for i, term in enumerate(terms):
        add(term, [term, z_in.at[i, 0], z_in.at[i, 1]])
    yield


def kernel(
    band, stu_in, tea_in, grad_out, stu_out, tea_out, loss,
    S, T, X, stu_other, grad, relay_a, relay_b, z, w, G, wide, xsq, xsq_other, part_sq, ysq_row, stu, tea, tall, ysq_tall,
    kept, row_l, col_l, sum_r, sum_c, pair_f, pair_b, others,
    a_far_out, a_near_out, a_far_in, a_near_in, a_x_out, a_x_in, a_x_relay, a_x_far,
    b_far_out, b_relay, b_x_out, b_x_in, b_x_far, b_z_far_out, b_z_far_in, b_z_out, b_z_in,
    send, recv, here,
):
    me = Place()
    mine = pl.multiple_of(me.h * ROWS, ROWS)
    other = pl.multiple_of((1 - me.h) * ROWS, ROWS)
    loads = [
        pltpu.make_async_copy(tea_in, T.at[me.s, me.h], here.at[0]),
        pltpu.make_async_copy(stu_in.at[pl.ds(mine, ROWS)], S.at[me.t], here.at[1]),
        pltpu.make_async_copy(stu_in.at[pl.ds(other, ROWS)], stu_other, here.at[2]),
        pltpu.make_async_copy(stu_in.at[pl.ds(other + GA, GB)], X.at[me.z], here.at[3]),
    ]
    for copy in loads:
        copy.start()
    barrier = pltpu.get_barrier_semaphore()
    peers = [me.outer()] + [me.at_row(d) for d in range(1, 8)] + [me.at_col(d) for d in range(1, 16)]
    for peer in peers:
        pl.semaphore_signal(barrier, inc=1, device_id=peer, device_id_type=MESH)

    def own_here():
        for copy in loads:
            copy.wait()
        pl.semaphore_wait(barrier, len(peers))

    wire = Wire(send, recv)
    gather(
        me, wire, stu_other, own_here, S, T, X, relay_a, relay_b, part_sq, ysq_row,
        cost_of(me, band, S, T, z, xsq, ysq_row),
    )
    sweeps(me, wire, z, wide, stu, tea, tall, row_l, col_l, kept, G.at[0], G.at[1])
    spread_lines(tea, tall)
    spread_lines(ysq_row, ysq_tall)
    make_plan(me, z, wide, tall, xsq, ysq_tall, w, sum_r, G.at[0], G.at[1])
    sums = tell(wire, sum_r, me.row_slot, 8, me.at_row)
    pair_f[me.h] = stu[...] / kappa
    sums.append(wire.start(pair_f.at[me.h], pair_f.at[me.h], me.partner()))
    tea[...] = tea[...] / kappa
    stores = [
        pltpu.make_async_copy(tea.at[aligned(me.h * LINES, LINES)], tea_out, here.at[4])
    ]
    stores[-1].start()
    pull = pull_of(S, T, w, wide, G)
    first = reduce_a(
        me, wire, G, pull, a_far_out, a_near_out, a_far_in, a_near_in,
        a_x_out, a_x_in, a_x_relay, a_x_far,
    )
    second = reduce_b(
        me, wire, G, pull, b_far_out, b_relay, b_x_out, b_x_in, b_x_far, others,
        b_z_far_out, b_z_far_in, b_z_out, b_z_in,
    )
    steps = [first, second] * 3 + [second, first, second, first]
    for number, step in enumerate(steps):
        next(step)
        if number == 1:
            for copy in sums:
                copy.wait_recv()
            summed = total_of([sum_r[i] for i in range(8)])
            sum_c[me.col_slot] = summed[LINES:, :]
            pair_b[me.h] = summed[:LINES, :]
            sums = tell(wire, sum_c, me.col_slot, 16, me.at_col)
            sums.append(wire.start(pair_b.at[me.h], pair_b.at[me.h], me.partner()))
            stores.append(pltpu.make_async_copy(pair_f, stu_out, here.at[5]))
            stores[-1].start()
        if number == 3:
            for copy in sums:
                copy.wait_recv()
            total = total_of([sum_c[i] for i in range(16)])
            total = jnp.sum(jnp.sum(total, axis=0, keepdims=True), axis=1, keepdims=True)
            loss[...] = total * (-1.0 / (kappa * TOKENS))
            spread_rows(pair_b.at[me.h], xsq)
            spread_rows(pair_b.at[1 - me.h], xsq_other)

    def finish(first_row, rows_total, own_terms, other_terms, at):
        size = 192 if rows_total % 192 == 0 else 224

        def block(r, carry):
            near = aligned(r * size, size)
            rows = pl.ds(pl.multiple_of(first_row + r * size, 32), size)
            own = pl.ds(pl.multiple_of(mine + first_row + r * size, 32), size)
            there = pl.ds(pl.multiple_of(other + first_row + r * size, 32), size)
            grad[own, :] = (
                xsq[rows, :] * S[me.t, rows, :].astype(f32)
                + total_of([term[near, :].astype(f32) for term in own_terms])
            )
            grad[there, :] = (
                xsq_other[rows, :] * stu_other[rows, :].astype(f32)
                + total_of([term[near, :].astype(f32) for term in other_terms])
            )
            return carry

        lax.fori_loop(0, rows_total // size, block, 0)
        for i, base in enumerate((mine, other)):
            rows = pl.ds(pl.multiple_of(base + first_row, 64), rows_total)
            stores.append(
                pltpu.make_async_copy(grad.at[rows], grad_out.at[rows], here.at[at + i])
            )
            stores[-1].start()

    finish(QA, QB, [G.at[me.t, pl.ds(QA, QB)]], [others.at[me.z]], 8)
    finish(0, QA, [G.at[me.t, pl.ds(0, QA)], a_x_far], [a_x_in.at[0], a_x_in.at[1]], 6)
    assert wire.used <= WIRES, wire.used
    wire.drain()
    for copy in stores:
        copy.wait()


def one_device(band_start, student, teacher):
    dma = pltpu.SemaphoreType.DMA
    vmem = pl.BlockSpec(memory_space=pltpu.VMEM)
    anywhere = pl.BlockSpec(memory_space=pl.ANY)

    def wide_bf16(*lead):
        return pltpu.VMEM((*lead, LANES), bf16)

    def wide_f32(*lead):
        return pltpu.VMEM((*lead, LANES), f32)

    scratch = [
        wide_bf16(16, ROWS),
        pltpu.VMEM((8, 2, PIECE, 2 * LANES), bf16),
        wide_bf16(4, GB),
        wide_bf16(ROWS),
        wide_f32(OWNED),
        wide_bf16(2, GA // 2),
        wide_bf16(4, 2, GB // 2),
        wide_f32(TILES, ROWS),
        pltpu.VMEM((ROWS, COLS), bf16),
        wide_f32(16, ROWS),
        wide_f32(ROWS),
        wide_f32(ROWS),
        wide_f32(ROWS),
        wide_f32(16, PIECE // LANES),
        wide_f32(TILES),
        wide_f32(LINES),
        wide_f32(TILES),
        wide_f32(TILES, 8),
        wide_f32(TILES, 8),
        wide_f32(2, TILES, 8),
        wide_f32(ITERS, 2, 8, LINES // 2),
        wide_f32(ITERS, 16, TILES),
        wide_f32(8, LINES + 8),
        wide_f32(16, 8),
        wide_f32(2, LINES),
        wide_f32(2, LINES),
        wide_f32(4, QB),
        wide_bf16(4, QA), wide_bf16(2, 4, QA), wide_bf16(4, 2, QA // 2), wide_bf16(2, 4, QA),
        wide_bf16(3, QA), wide_bf16(2, QA), wide_bf16(2, QA // 2), wide_bf16(QA),
        wide_bf16(4, QB), wide_bf16(4, 2, QB // 2), wide_bf16(2, 4, QB), wide_bf16(2, 4, QB),
        wide_bf16(4, QB),
        wide_bf16(2, QB), wide_bf16(2, 2, QB // 2), wide_bf16(2, 2, QB), wide_bf16(2, 2, QB),
        dma((WIRES,)),
        dma((WIRES,)),
        dma((10,)),
    ]
    return pl.pallas_call(
        kernel,
        out_shape=(
            jax.ShapeDtypeStruct((OWNED, LANES), f32),
            jax.ShapeDtypeStruct((2, LINES, LANES), f32),
            jax.ShapeDtypeStruct((LINES, LANES), f32),
            jax.ShapeDtypeStruct((1, 1), f32),
        ),
        in_specs=[pl.BlockSpec(memory_space=pltpu.SMEM), anywhere, anywhere],
        out_specs=(anywhere, anywhere, anywhere, vmem),
        scratch_shapes=scratch,
        compiler_params=pltpu.CompilerParams(
            collective_id=0, has_side_effects=True, vmem_limit_bytes=62 * 2**20
        ),
    )(band_start, student, teacher)


def local(student, teacher, band_start):
    grad, stu, tea, loss = one_device(band_start, student, teacher)
    return (grad, stu.reshape(OWNED), tea.reshape(PIECE), loss.reshape(()))


def solution(mesh):
    placed = (P("stu", "tea"), P("tea", "stu"), P())
    return jax.shard_map(
        local,
        mesh=mesh,
        in_specs=placed,
        out_specs=(P("stu", "tea"), P("stu"), P("tea"), P()),
        check_vma=False,
    )
```

```python
import functools
import math

import jax
import jax.numpy as jnp
from jax import lax
from jax.experimental import pallas as pl
from jax.experimental.pallas import tpu as pltpu
from jax.sharding import PartitionSpec as P

D = 2048
BLK = 512
W = 4
ITERS = 3
LANES = 128
OWNED = 2048
ROWS = 1024
COLS = 2048
PIECE = 1024
TILES = COLS // LANES
LINES = ROWS // LANES
TOKENS = 16384
GA, GB = 896, 128
QA, QB = 576, 448
WIRES = 300
UP, DOWN = 1, 3

epsilon = 0.02
kappa = math.log2(math.e) / epsilon
log2e = math.log2(math.e)
log2_tokens = math.log2(TOKENS)
unlisted = -1e30
MESH = pl.DeviceIdType.MESH
f32 = jnp.float32
bf16 = jnp.bfloat16


def aligned(start, size):
    return pl.ds(pl.multiple_of(start, size), size)


def total_of(parts):
    return functools.reduce(lambda a, b: a + b, parts)


def merge(parts):
    highest = functools.reduce(jnp.maximum, parts)
    return highest + jnp.log(total_of([jnp.exp2(p - highest) for p in parts])) * log2e


class Place:
    def __init__(self):
        self.s = lax.axis_index("stu")
        self.t = lax.axis_index("tea")
        self.y = lax.div(self.s, 2)
        self.core = lax.rem(self.s, 2)
        self.z = lax.div(self.t, 4)
        self.x = lax.rem(self.t, 4)
        self.h = lax.rem(self.x, 2)
        self.l = lax.div(self.x, 2)
        self.row_slot = 2 * self.z + self.l
        self.col_slot = 2 * self.s + self.h

    def zi(self, dz):
        return lax.rem(self.z + dz, 4)

    def yi(self, dy):
        return lax.rem(self.y + dy, 4)

    def xi(self, dx):
        return lax.rem(self.x + dx, 4)

    def tea(self, dz, dx):
        return self.zi(dz) * 4 + self.xi(dx)

    def stu(self, dy):
        return lax.rem(self.y + dy, 4) * 2 + self.core

    def at_x(self, d):
        return (self.s, self.tea(0, d))

    def at_z(self, d):
        return (self.s, self.tea(d, 0))

    def at_y(self, d):
        return (self.stu(d), self.t)

    def sibling(self):
        return (self.y * 2 + 1 - self.core, self.t)

    def partner(self):
        return (self.s, self.z * 4 + self.l * 2 + 1 - self.h)

    def outer(self):
        return (self.s, self.z * 4 + lax.rem(self.x + 3 + 2 * self.h, 4))

    def at_row(self, d):
        k = lax.rem(self.row_slot + d, 8)
        return (self.s, lax.div(k, 2) * 4 + lax.rem(k, 2) * 2 + self.h)

    def at_col(self, d):
        k = lax.rem(self.col_slot + d, 16)
        return (lax.div(k, 2), self.z * 4 + self.l * 2 + lax.rem(k, 2))


class Wire:
    def __init__(self, send, recv):
        self.send, self.recv, self.used, self.open = send, recv, 0, []

    def start(self, src, dst, device):
        copy = pltpu.make_async_remote_copy(
            src_ref=src, dst_ref=dst,
            send_sem=self.send.at[self.used], recv_sem=self.recv.at[self.used],
            device_id=device, device_id_type=MESH,
        )
        self.used += 1
        copy.start()
        self.open.append(copy)
        return copy

    def drain(self):
        for copy in self.open:
            copy.wait_send()
        self.open = []


WAYS = ((UP, DOWN, 0), (DOWN, UP, 1))


def gather(me, wire, stu_other, own_here, S, T, X, relay_a, relay_b, part_sq, ysq_row, cost):
    A, B = pl.ds(0, GA), pl.ds(GA, GB)
    a_part = [pl.ds(0, GA // 2), pl.ds(GA // 2, GA // 2)]
    b_part = [pl.ds(GA, GB // 2), pl.ds(GA + GB // 2, GB // 2)]
    x_part = [pl.ds(0, GB // 2), pl.ds(GB // 2, GB // 2)]
    t_part = [pl.ds(0, PIECE // 2), pl.ds(PIECE // 2, PIECE // 2)]

    def push(ref, device):
        return wire.start(ref, ref, device)

    def piece(dz, dx, rows):
        return S.at[me.tea(dz, dx), rows]

    def t_push(dy, e, rows, device):
        return push(T.at[me.stu(dy), e, rows], device)

    own, other = me.h, 1 - me.h
    ty, tyf = {}, {0: [], 1: []}
    tc = {(order, d): [] for order in range(2) for d in (0, UP, DOWN, 2)}

    def t_spread(order, e, parts):
        for keep in parts:
            way = WAYS[keep][0]
            ty[order, way, 0] = t_push(0, e, t_part[keep], me.at_y(way))
        for keep in parts:
            way = WAYS[1 - keep][0]
            ty[order, way, 1] = t_push(0, e, t_part[keep], me.at_y(way))
            tc[order, 0].append(t_push(0, e, t_part[keep], me.sibling()))

    own_here()
    ax, ar, axf, az, azf = {}, {}, {}, {}, []
    bz, bzf, bx, br, bxf = {}, [], {}, {}, {}
    for way, back, keep in WAYS:
        ar[way] = wire.start(S.at[me.t, a_part[keep]], relay_a.at[keep], me.at_x(way))
    t_spread(0, own, (0, 1))
    for way, back, keep in WAYS:
        ax[way] = wire.start(stu_other.at[A], S.at[me.t, A], me.at_x(way))
    tp = [t_push(0, own, t_part[0], me.partner())]

    def turn_a(dx):
        for way, back, keep in WAYS:
            az[dx, way, 0] = push(piece(0, dx, a_part[keep]), me.at_z(way))
        for way, back, keep in WAYS:
            az[dx, way, 1] = push(piece(0, dx, a_part[1 - keep]), me.at_z(way))

    def turn_b(dz):
        for way, back, keep in WAYS:
            br[dz, way] = wire.start(
                piece(dz, 0, b_part[keep]), relay_b.at[me.zi(dz), keep], me.at_x(way)
            )
        for way in (UP, DOWN):
            bx[dz, way] = wire.start(X.at[me.zi(dz)], piece(dz, 0, B), me.at_x(way))

    turn_a(0)
    own_squares(me, T, part_sq)
    squares = tell(wire, part_sq, me.col_slot, 16, me.at_col)
    for way in (UP, DOWN):
        bz[way] = (push(piece(0, 0, B), me.at_z(way)), push(X.at[me.z], me.at_z(way)))

    for way, back, keep in WAYS:
        ar[way].wait_recv()
        axf[way] = wire.start(relay_a.at[keep], piece(0, back, a_part[keep]), me.at_x(way))
    for way, back, keep in WAYS:
        ax[way].wait_recv()
        turn_a(back)
    tp.append(t_push(0, own, t_part[1], me.partner()))

    def t_far(order, e, keep):
        way, back, _ = WAYS[keep]
        ty[order, way, 0].wait_recv()
        tyf[order].append(t_push(back, e, t_part[keep], me.at_y(way)))

    def t_whole(order, e):
        for way, back, keep in WAYS:
            ty[order, way, 1].wait_recv()
            tc[order, back].append(t_push(back, e, pl.ds(0, PIECE), me.sibling()))

    def t_last(order, e):
        for keep, copy in enumerate(tyf[order]):
            copy.wait_recv()
            tc[order, 2].append(t_push(2, e, t_part[keep], me.sibling()))

    for way, back, keep in WAYS:
        for copy in bz[way]:
            copy.wait_recv()
        bzf.append(push(piece(back, 0, b_part[keep]), me.at_z(way)))
        bzf.append(push(X.at[me.zi(back), x_part[keep]], me.at_z(way)))
    for copy in axf.values():
        copy.wait_recv()
    turn_a(2)
    tp[0].wait_recv()
    t_spread(1, other, (0,))
    t_far(0, own, 0)
    t_far(0, own, 1)
    t_whole(0, own)
    tp[1].wait_recv()
    t_spread(1, other, (1,))
    turn_b(0)
    turn_b(DOWN)
    turn_b(UP)
    for copy in bzf:
        copy.wait_recv()
    turn_b(2)

    def b_relay(dz):
        bxf[dz] = []
        for way, back, keep in WAYS:
            br[dz, way].wait_recv()
            bxf[dz].append(
                wire.start(relay_b.at[me.zi(dz), keep], piece(dz, back, b_part[keep]), me.at_x(way))
            )

    def a_relay(dx):
        for way, back, keep in WAYS:
            az[dx, way, 0].wait_recv()
            azf.append(push(piece(back, dx, a_part[keep]), me.at_z(way)))

    def b_here(dz):
        for way in (UP, DOWN):
            bx[dz, way].wait_recv()
        for copy in bxf[dz]:
            copy.wait_recv()

    def t_here(order, *places):
        for d in places:
            for copy in tc[order, d]:
                copy.wait_recv()

    def a_here(*places):
        for dx in places:
            for way in (UP, DOWN):
                az[dx, way, 1].wait_recv()

    a_relay(0)
    t_last(0, own)
    a_relay(DOWN)
    a_relay(UP)
    t_far(1, other, 0)
    b_relay(0)
    b_relay(DOWN)
    b_relay(UP)
    t_here(0, 0, UP, DOWN, 2)
    b_here(0)
    a_relay(2)
    t_far(1, other, 1)
    cost([me.zi(0)], own, first=True)
    b_relay(2)
    t_whole(1, other)
    a_here(0, UP, DOWN, 2)
    b_here(DOWN)
    b_here(UP)
    cost([me.zi(DOWN), me.zi(UP)], own)
    for copy in azf + squares:
        copy.wait_recv()
    for e in range(2):
        ysq_row[e * PIECE // LANES:(e + 1) * PIECE // LANES, :] = total_of(
            [part_sq[2 * i + e] for i in range(8)]
        )
    b_here(2)
    cost([me.zi(2)], own, last=True, new_rows=True)
    t_last(1, other)
    t_here(1, 0, UP, DOWN)
    cost([me.yi(0), me.yi(DOWN), me.yi(UP)], other, first=True)
    t_here(1, 2)
    cost([me.yi(2)], other, last=True)


def own_squares(me, T, part_sq):
    def block(b, carry):
        rows = aligned(b * LANES, LANES)
        squared = total_of([
            jnp.square(T[me.s, me.h, rows, side * LANES:(side + 1) * LANES].astype(f32))
            for side in range(2)
        ])
        part_sq[me.col_slot, pl.ds(b, 1), :] = jnp.sum(squared.T, axis=0, keepdims=True)
        return carry

    lax.fori_loop(0, PIECE // LANES, block, 0)


def cost_of(me, band, S, T, z, xsq, ysq_row):
    scale = kappa / D

    def cost(groups, e, first=False, last=False, new_rows=False):
        def cols_block(n, carry):
            cols = aligned(n * 256, 256)
            rhs = jnp.concatenate(
                [T[2 * group + i, e, cols, :] for group in groups for i in range(2)], axis=1
            )
            lhs = jnp.concatenate(
                [S[4 * group + i] for group in groups for i in range(4)], axis=1
            )
            prod = lax.dot_general(
                lhs, rhs, (((1,), (1,)), ((), ())), preferred_element_type=f32
            )
            for side in range(2):
                at = e * (TILES // 2) + 2 * n + side
                block = me.row_slot * 4 + e * 2 + lax.div(n, 2)
                for half in range(2):
                    rows = pl.ds(half * BLK, BLK)
                    tile = prod[half * BLK:(half + 1) * BLK, side * LANES:(side + 1) * LANES]
                    tile = tile if first else z[at, rows, :] + tile
                    if last:
                        lowest = band[me.s * 4 + me.h * 2 + half]
                        lowest = jnp.full((BLK, LANES), lowest, jnp.int32)
                        here = jnp.full((BLK, LANES), block, jnp.int32)
                        listed = (here >= lowest) & (here < lowest + W)
                        tile = (2.0 * tile - xsq[rows, :] - ysq_row[pl.ds(at, 1), :]) * scale
                        tile = jnp.where(listed, tile, unlisted)
                    z[at, rows, :] = tile
            return carry

        def squares_block(b, carry):
            rows = aligned(b * LANES, LANES)
            squared = total_of([jnp.square(S[i, rows, :].astype(f32)) for i in range(16)])
            xsq[rows, :] = jnp.broadcast_to(
                jnp.sum(squared, axis=1, keepdims=True), (LANES, LANES)
            )
            return carry

        if new_rows:
            lax.fori_loop(0, LINES, squares_block, 0)
        lax.fori_loop(0, PIECE // 256, cols_block, 0)

    return cost


def spread_lines(compact, tall):
    for c in range(TILES):
        tall[c] = jnp.broadcast_to(compact[c:c + 1, :], (8, LANES))


def row_stats(z, tall, half, lane_high, lane_total, put):
    def lanes(b, carry):
        for part in range(4):
            rows = aligned(b * 64 + part * 16, 16)
            scores = [z[c, rows, :].reshape(2, 8, LANES) + tall[c][None] for c in range(TILES)]
            high = functools.reduce(jnp.maximum, scores)
            lane_high[rows, :] = high.reshape(16, LANES)
            lane_total[rows, :] = total_of([jnp.exp2(v - high) for v in scores]).reshape(16, LANES)
        return carry

    lax.fori_loop(half * (ROWS // 128), (half + 1) * (ROWS // 128), lanes, 0)

    def block(b, carry):
        rows = aligned((half * (LINES // 2) + b) * LANES, LANES)
        value = (lane_high[rows, :] + jnp.log(lane_total[rows, :]) * log2e).T
        top = jnp.max(value, axis=0, keepdims=True)
        total = jnp.sum(jnp.exp2(value - top), axis=0, keepdims=True)
        put(b, top + jnp.log(total) * log2e)
        return carry

    lax.fori_loop(0, LINES // 2, block, 0, unroll=True)


def spread_rows(compact, wide, first=0, count=LINES):
    for b in range(first, first + count):
        line = jnp.broadcast_to(compact[b:b + 1, :], (LANES, LANES))
        wide[b * LANES:(b + 1) * LANES, :] = line.T


def col_stats(z, wide, half, kept, put):
    def tiles(cc, carry):
        if half == 0:
            highs = [jnp.full((8, LANES), unlisted, f32) for _ in range(4)]
            totals = [jnp.zeros((8, LANES), f32) for _ in range(4)]
        else:
            highs = [kept[0, cc * 4 + k] for k in range(4)]
            totals = [kept[1, cc * 4 + k] for k in range(4)]
        for b in range(ROWS // 128):
            rows = pl.ds(half * (ROWS // 2) + b * 64, 64)
            pot = wide[rows, :]
            for k in range(4):
                scores = (z[cc * 4 + k, rows, :] + pot).reshape(8, 8, LANES)
                new = jnp.maximum(highs[k], jnp.max(scores, axis=0))
                totals[k] = totals[k] * jnp.exp2(highs[k] - new) + jnp.sum(
                    jnp.exp2(scores - new[None]), axis=0
                )
                highs[k] = new
        for k in range(4):
            if half == 0:
                kept[0, cc * 4 + k] = highs[k]
                kept[1, cc * 4 + k] = totals[k]
                continue
            top = jnp.max(highs[k], axis=0, keepdims=True)
            total = jnp.sum(totals[k] * jnp.exp2(highs[k] - top), axis=0, keepdims=True)
            put(cc * 4 + k, top + jnp.log(total) * log2e)
        return carry

    lax.fori_loop(0, TILES // 4, tiles, 0)


def tell(wire, slots, index, count, peer):
    return [wire.start(slots.at[index], slots.at[index], peer(d)) for d in range(1, count)]


def swap(wire, slots, index, count, peer):
    for copy in tell(wire, slots, index, count, peer):
        copy.wait_recv()


def sweeps(me, wire, z, wide, stu, tea, tall, row_l, col_l, kept, lane_high, lane_total):
    tea[...] = jnp.zeros_like(tea)
    for sweep in range(ITERS):
        spread_lines(tea, tall)
        rows_sent = []
        for half in range(2):
            rl = row_l.at[sweep, half]

            def put_row(b, value):
                rl[me.row_slot, pl.ds(b, 1), :] = value

            row_stats(z, tall, half, lane_high, lane_total, put_row)
            rows_sent.append(tell(wire, rl, me.row_slot, 8, me.at_row))
        cl = col_l.at[sweep]

        def put_col(c, value):
            cl[me.col_slot, pl.ds(c, 1), :] = value

        for half in range(2):
            rl = row_l.at[sweep, half]
            for copy in rows_sent[half]:
                copy.wait_recv()
            first = half * (LINES // 2)
            stu[first:first + LINES // 2, :] = -log2_tokens - merge([rl[i] for i in range(8)])
            spread_rows(stu, wide, first, LINES // 2)
            col_stats(z, wide, half, kept, put_col)
        swap(wire, cl, me.col_slot, 16, me.at_col)
        tea[...] = -log2_tokens - merge([cl[i] for i in range(16)])


def make_plan(me, z, wide, tall, xsq, ysq_tall, w, sum_r, lane_mass, lane_pull):
    def lanes(b, loss):
        for part in range(4):
            rows = aligned(b * 64 + part * 16, 16)
            pot = (wide[rows, :] + log2_tokens).reshape(2, 8, LANES)
            mass, pull = [], []
            for c in range(TILES):
                tile = z[c, rows, :].reshape(2, 8, LANES)
                scaled = jnp.exp2(tile + pot + tall[c][None])
                loss = loss + total_of([scaled[i] * tile[i] for i in range(2)])
                rounded = scaled.reshape(16, LANES).astype(bf16)
                w[rows, c * LANES:(c + 1) * LANES] = rounded
                rounded = rounded.astype(f32).reshape(2, 8, LANES)
                mass.append(rounded)
                pull.append(rounded * (ysq_tall[c][None] + (D / kappa) * tile))
            lane_mass[rows, :] = total_of(mass).reshape(16, LANES)
            lane_pull[rows, :] = total_of(pull).reshape(16, LANES)
        return loss

    loss = lax.fori_loop(0, ROWS // 64, lanes, jnp.zeros((8, LANES), f32))

    def block(b, carry):
        rows = aligned(b * LANES, LANES)
        mass = jnp.sum(lane_mass[rows, :].T, axis=0, keepdims=True)
        pull = jnp.sum(lane_pull[rows, :].T, axis=0, keepdims=True)
        own = xsq[rows, :].T[0:1, :]
        usable = own > 1e-20
        gamma = jnp.where(usable, 0.5 * (mass + pull / jnp.where(usable, own, 1.0)), 0.0)
        wide[rows, :] = jnp.broadcast_to(gamma, (LANES, LANES)).T
        sum_r[me.row_slot, pl.ds(b, 1), :] = mass - gamma
        return carry

    lax.fori_loop(0, LINES, block, 0, unroll=True)
    sum_r[me.row_slot, LINES:LINES + 8, :] = loss


def pull_of(S, T, w, wide, G):
    def pull(q, part):
        def rows_block(rows):
            prod = jnp.dot(
                w[rows, :], T[q].reshape(COLS, 2 * LANES), preferred_element_type=f32
            )
            gamma = wide[rows, :]
            for side in range(2):
                own = S[2 * q + side, rows, :].astype(f32)
                G[2 * q + side, rows, :] = gamma * own - prod[:, side * LANES:(side + 1) * LANES]

        if part == 0:
            def block(r, carry):
                rows_block(aligned(r * (QA // 2), QA // 2))
                return carry

            lax.fori_loop(0, 2, block, 0)
        else:
            rows_block(pl.ds(QA, QB))

    return pull


def add(dst, terms):
    size = 96 if dst.shape[0] % 96 == 0 else 112

    def block(r, carry):
        rows = aligned(r * size, size)
        dst[rows, :] = total_of([term[rows, :].astype(f32) for term in terms]).astype(dst.dtype)
        return carry

    lax.fori_loop(0, dst.shape[0] // size, block, 0)


def in_two(rows):
    return (pl.ds(0, rows // 2), pl.ds(rows // 2, rows // 2))


def reduce_a(me, wire, G, pull, far_out, near_out, far_in, near_in, x_out, x_in, x_relay, x_far):
    PARTS = in_two(QA)

    def value(t):
        return G.at[t, pl.ds(0, QA)]

    def pull_to(dz):
        for k in range(2):
            pull(2 * me.zi(dz) + k, 0)

    pull_to(2)
    far = []
    for j in range(4):
        add(far_out.at[j], [value(me.zi(2) * 4 + j)])
        far.append([
            wire.start(far_out.at[j, PARTS[keep]], far_in.at[j, keep], me.at_z(way))
            for way, back, keep in WAYS
        ])
    yield
    pull_to(UP)
    pull_to(DOWN)
    near = []
    for j in range(4):
        for way, back, keep in WAYS:
            far[j][keep].wait_recv()
            chained, direct = PARTS[keep], PARTS[1 - keep]
            mine = value(me.zi(way) * 4 + j)
            out = near_out.at[keep, j]
            add(out.at[chained], [mine.at[chained], far_in.at[j, keep]])
            add(out.at[direct], [mine.at[direct]])
            near.append(wire.start(out, near_in.at[keep, j], me.at_z(way)))
    yield
    pull_to(0)
    for copy in near:
        copy.wait_recv()
    for j in range(4):
        mine = value(me.z * 4 + j)
        add(mine, [mine, near_in.at[0, j], near_in.at[1, j]])
    add(x_out.at[2], [value(me.tea(0, 2))])
    far = [
        wire.start(x_out.at[2, PARTS[keep]], x_relay.at[keep], me.at_x(way))
        for way, back, keep in WAYS
    ]
    near = []
    for way, back, keep in WAYS:
        add(x_out.at[keep], [value(me.tea(0, way))])
        near.append(wire.start(x_out.at[keep], x_in.at[keep], me.at_x(way)))
    yield
    last = []
    for way, back, keep in WAYS:
        far[keep].wait_recv()
        last.append(wire.start(x_relay.at[keep], x_far.at[PARTS[keep]], me.at_x(way)))
    yield
    for copy in near + last:
        copy.wait_recv()
    yield


def reduce_b(
    me, wire, G, pull, far_out, relay, x_out, x_in, x_far, others,
    z_far_out, z_far_in, z_out, z_in,
):
    PARTS = in_two(QB)
    order = (2, UP, DOWN, 0)

    def value(t):
        return G.at[t, pl.ds(QA, QB)]

    far, near, last = {}, {}, {}
    for dz in order:
        pull(2 * me.zi(dz) + 1 - me.l, 1)
        add(far_out.at[me.zi(dz)], [value(me.tea(dz, 2))])
        far[dz] = [
            wire.start(
                far_out.at[me.zi(dz), PARTS[keep]], relay.at[me.zi(dz), keep], me.at_x(way)
            )
            for way, back, keep in WAYS
        ]
    yield
    for dz in order:
        pull(2 * me.zi(dz) + me.l, 1)
        near[dz] = []
        for way, back, keep in WAYS:
            add(x_out.at[keep, me.zi(dz)], [value(me.tea(dz, way))])
            near[dz].append(
                wire.start(x_out.at[keep, me.zi(dz)], x_in.at[keep, me.zi(dz)], me.at_x(way))
            )
        last[dz] = []
        for way, back, keep in WAYS:
            far[dz][keep].wait_recv()
            last[dz].append(
                wire.start(relay.at[me.zi(dz), keep], x_far.at[me.zi(dz), PARTS[keep]], me.at_x(way))
            )
    yield

    def arrived(dz):
        for copy in near[dz] + last[dz]:
            copy.wait_recv()
        mine, other = value(me.tea(dz, 0)), others.at[me.zi(dz)]
        add(mine, [mine, x_far.at[me.zi(dz)]])
        add(other, [x_in.at[0, me.zi(dz)], x_in.at[1, me.zi(dz)]])
        return mine, other

    z_far = {}
    for i, term in enumerate(arrived(2)):
        add(z_far_out.at[i], [term])
        for way, back, keep in WAYS:
            z_far[i, way] = wire.start(
                z_far_out.at[i, PARTS[keep]], z_far_in.at[i, keep], me.at_z(way)
            )
    yield
    z_near = []
    terms = {way: arrived(way) for way in (UP, DOWN)}
    for i in range(2):
        for way, back, keep in WAYS:
            z_far[i, way].wait_recv()
            chained, direct = PARTS[keep], PARTS[1 - keep]
            term, out = terms[way][i], z_out.at[i, keep]
            add(out.at[chained], [term.at[chained], z_far_in.at[i, keep]])
            add(out.at[direct], [term.at[direct]])
            z_near.append(wire.start(out, z_in.at[i, keep], me.at_z(way)))
    yield
    terms = arrived(0)
    for copy in z_near:
        copy.wait_recv()
    for i, term in enumerate(terms):
        add(term, [term, z_in.at[i, 0], z_in.at[i, 1]])
    yield


def kernel(
    band, stu_in, tea_in, grad_out, stu_out, tea_out, loss,
    S, T, X, stu_other, grad, relay_a, relay_b, z, w, G, wide, xsq, xsq_other, part_sq, ysq_row, stu, tea, tall, ysq_tall,
    kept, row_l, col_l, sum_r, sum_c, pair_f, pair_b, others,
    a_far_out, a_near_out, a_far_in, a_near_in, a_x_out, a_x_in, a_x_relay, a_x_far,
    b_far_out, b_relay, b_x_out, b_x_in, b_x_far, b_z_far_out, b_z_far_in, b_z_out, b_z_in,
    send, recv, here,
):
    me = Place()
    mine = pl.multiple_of(me.h * ROWS, ROWS)
    other = pl.multiple_of((1 - me.h) * ROWS, ROWS)
    loads = [
        pltpu.make_async_copy(tea_in, T.at[me.s, me.h], here.at[0]),
        pltpu.make_async_copy(stu_in.at[pl.ds(mine, ROWS)], S.at[me.t], here.at[1]),
        pltpu.make_async_copy(stu_in.at[pl.ds(other, ROWS)], stu_other, here.at[2]),
        pltpu.make_async_copy(stu_in.at[pl.ds(other + GA, GB)], X.at[me.z], here.at[3]),
    ]
    for copy in loads:
        copy.start()
    barrier = pltpu.get_barrier_semaphore()
    peers = [me.outer()] + [me.at_row(d) for d in range(1, 8)] + [me.at_col(d) for d in range(1, 16)]
    for peer in peers:
        pl.semaphore_signal(barrier, inc=1, device_id=peer, device_id_type=MESH)

    def own_here():
        for copy in loads:
            copy.wait()
        pl.semaphore_wait(barrier, len(peers))

    wire = Wire(send, recv)
    gather(
        me, wire, stu_other, own_here, S, T, X, relay_a, relay_b, part_sq, ysq_row,
        cost_of(me, band, S, T, z, xsq, ysq_row),
    )
    sweeps(me, wire, z, wide, stu, tea, tall, row_l, col_l, kept, G.at[0], G.at[1])
    spread_lines(tea, tall)
    spread_lines(ysq_row, ysq_tall)
    make_plan(me, z, wide, tall, xsq, ysq_tall, w, sum_r, G.at[0], G.at[1])
    sums = tell(wire, sum_r, me.row_slot, 8, me.at_row)
    pair_f[me.h] = stu[...] / kappa
    sums.append(wire.start(pair_f.at[me.h], pair_f.at[me.h], me.partner()))
    tea[...] = tea[...] / kappa
    stores = [
        pltpu.make_async_copy(tea.at[aligned(me.h * LINES, LINES)], tea_out, here.at[4])
    ]
    stores[-1].start()
    pull = pull_of(S, T, w, wide, G)
    first = reduce_a(
        me, wire, G, pull, a_far_out, a_near_out, a_far_in, a_near_in,
        a_x_out, a_x_in, a_x_relay, a_x_far,
    )
    second = reduce_b(
        me, wire, G, pull, b_far_out, b_relay, b_x_out, b_x_in, b_x_far, others,
        b_z_far_out, b_z_far_in, b_z_out, b_z_in,
    )
    steps = [first, second] * 3 + [second, first, second, first]
    for number, step in enumerate(steps):
        next(step)
        if number == 1:
            for copy in sums:
                copy.wait_recv()
            summed = total_of([sum_r[i] for i in range(8)])
            sum_c[me.col_slot] = summed[LINES:, :]
            pair_b[me.h] = summed[:LINES, :]
            sums = tell(wire, sum_c, me.col_slot, 16, me.at_col)
            sums.append(wire.start(pair_b.at[me.h], pair_b.at[me.h], me.partner()))
            stores.append(pltpu.make_async_copy(pair_f, stu_out, here.at[5]))
            stores[-1].start()
        if number == 3:
            for copy in sums:
                copy.wait_recv()
            total = total_of([sum_c[i] for i in range(16)])
            total = jnp.sum(jnp.sum(total, axis=0, keepdims=True), axis=1, keepdims=True)
            loss[...] = total * (-1.0 / (kappa * TOKENS))
            spread_rows(pair_b.at[me.h], xsq)
            spread_rows(pair_b.at[1 - me.h], xsq_other)

    def finish(first_row, rows_total, own_terms, other_terms, at):
        size = 192 if rows_total % 192 == 0 else 224

        def block(r, carry):
            near = aligned(r * size, size)
            rows = pl.ds(pl.multiple_of(first_row + r * size, 32), size)
            own = pl.ds(pl.multiple_of(mine + first_row + r * size, 32), size)
            there = pl.ds(pl.multiple_of(other + first_row + r * size, 32), size)
            grad[own, :] = (
                xsq[rows, :] * S[me.t, rows, :].astype(f32)
                + total_of([term[near, :].astype(f32) for term in own_terms])
            )
            grad[there, :] = (
                xsq_other[rows, :] * stu_other[rows, :].astype(f32)
                + total_of([term[near, :].astype(f32) for term in other_terms])
            )
            return carry

        lax.fori_loop(0, rows_total // size, block, 0)
        for i, base in enumerate((mine, other)):
            rows = pl.ds(pl.multiple_of(base + first_row, 64), rows_total)
            stores.append(
                pltpu.make_async_copy(grad.at[rows], grad_out.at[rows], here.at[at + i])
            )
            stores[-1].start()

    finish(QA, QB, [G.at[me.t, pl.ds(QA, QB)]], [others.at[me.z]], 8)
    finish(0, QA, [G.at[me.t, pl.ds(0, QA)], a_x_far], [a_x_in.at[0], a_x_in.at[1]], 6)
    assert wire.used <= WIRES, wire.used
    wire.drain()
    for copy in stores:
        copy.wait()


def one_device(band_start, student, teacher):
    dma = pltpu.SemaphoreType.DMA
    vmem = pl.BlockSpec(memory_space=pltpu.VMEM)
    anywhere = pl.BlockSpec(memory_space=pl.ANY)

    def wide_bf16(*lead):
        return pltpu.VMEM((*lead, LANES), bf16)

    def wide_f32(*lead):
        return pltpu.VMEM((*lead, LANES), f32)

    scratch = [
        wide_bf16(16, ROWS),
        pltpu.VMEM((8, 2, PIECE, 2 * LANES), bf16),
        wide_bf16(4, GB),
        wide_bf16(ROWS),
        wide_f32(OWNED),
        wide_bf16(2, GA // 2),
        wide_bf16(4, 2, GB // 2),
        wide_f32(TILES, ROWS),
        pltpu.VMEM((ROWS, COLS), bf16),
        wide_f32(16, ROWS),
        wide_f32(ROWS),
        wide_f32(ROWS),
        wide_f32(ROWS),
        wide_f32(16, PIECE // LANES),
        wide_f32(TILES),
        wide_f32(LINES),
        wide_f32(TILES),
        wide_f32(TILES, 8),
        wide_f32(TILES, 8),
        wide_f32(2, TILES, 8),
        wide_f32(ITERS, 2, 8, LINES // 2),
        wide_f32(ITERS, 16, TILES),
        wide_f32(8, LINES + 8),
        wide_f32(16, 8),
        wide_f32(2, LINES),
        wide_f32(2, LINES),
        wide_f32(4, QB),
        wide_bf16(4, QA), wide_bf16(2, 4, QA), wide_bf16(4, 2, QA // 2), wide_bf16(2, 4, QA),
        wide_bf16(3, QA), wide_bf16(2, QA), wide_bf16(2, QA // 2), wide_bf16(QA),
        wide_bf16(4, QB), wide_bf16(4, 2, QB // 2), wide_bf16(2, 4, QB), wide_bf16(2, 4, QB),
        wide_bf16(4, QB),
        wide_bf16(2, QB), wide_bf16(2, 2, QB // 2), wide_bf16(2, 2, QB), wide_bf16(2, 2, QB),
        dma((WIRES,)),
        dma((WIRES,)),
        dma((10,)),
    ]
    return pl.pallas_call(
        kernel,
        out_shape=(
            jax.ShapeDtypeStruct((OWNED, LANES), f32),
            jax.ShapeDtypeStruct((2, LINES, LANES), f32),
            jax.ShapeDtypeStruct((LINES, LANES), f32),
            jax.ShapeDtypeStruct((1, 1), f32),
        ),
        in_specs=[pl.BlockSpec(memory_space=pltpu.SMEM), anywhere, anywhere],
        out_specs=(anywhere, anywhere, anywhere, vmem),
        scratch_shapes=scratch,
        compiler_params=pltpu.CompilerParams(
            collective_id=0, has_side_effects=True, vmem_limit_bytes=62 * 2**20
        ),
    )(band_start, student, teacher)


def local(student, teacher, band_start):
    grad, stu, tea, loss = one_device(band_start, student, teacher)
    return (grad, stu.reshape(OWNED), tea.reshape(PIECE), loss.reshape(()))


def solution(mesh):
    placed = (P("stu", "tea"), P("tea", "stu"), P())
    return jax.shard_map(
        local,
        mesh=mesh,
        in_specs=placed,
        out_specs=(P("stu", "tea"), P("stu"), P("tea"), P()),
        check_vma=False,
    )
```
